32 devices in a mesh: shard: 4 (over z), context: 2 (over x), tensor: 4 (over y, core).
Axes of the slice: x: 2, y: 2, z: 4, core: 2. Of those that a mesh axis runs over, the one named last changes fastest.
Arguments:
- prompt_tokens: bfloat16 [8, 2048, 1280], P('shard', 'context'), may hold values from -18 to 18, as said below
- later_tokens: bfloat16 [8, 8, 256, 1280], P('shard', 'context'), may hold values from -18 to 18, as said below
- prompt_upstream: bfloat16 [8, 2048, 1280], P('shard', 'context'), may hold values from -6 to 6
- later_upstream: bfloat16 [8, 8, 256, 1280], P('shard', 'context'), may hold values from -6 to 6
- prompt_lengths: int32 [8], P('shard'), may hold values from 1536 to 2048
- later_lengths: int32 [8, 8], P('shard', 'context'), may hold values from 64 to 256
- query_weight: bfloat16 [1280, 1280], P(('shard', 'context'), 'tensor'), may hold values from -0.15625 to 0.15625
- key_weight: bfloat16 [1280, 1280], P(('shard', 'context'), 'tensor'), may hold values from -0.15625 to 0.15625
- value_weight: bfloat16 [1280, 1280], P(('shard', 'context'), 'tensor'), may hold values from -0.15625 to 0.15625
- out_weight: bfloat16 [1280, 1280], P('tensor', ('shard', 'context')), may hold values from -2 to 2
- up_weight: bfloat16 [1280, 1280], P(('shard', 'context'), 'tensor'), may hold values from -1 to 1
- down_weight: bfloat16 [1280, 1280], P('tensor', ('shard', 'context')), may hold values from -0.15625 to 0.15625
- pre_gain: bfloat16 [1280], P(('shard', 'context')), may hold values from 0.099609375 to 1.8984375
- pre_shift: bfloat16 [1280], P(('shard', 'context')), may hold values from -4 to 4
- mid_gain: bfloat16 [1280], P(('shard', 'context')), may hold values from 0.099609375 to 1.8984375
- mid_shift: bfloat16 [1280], P(('shard', 'context')), may hold values from -4 to 4
- query_bias: bfloat16 [1280], P('tensor'), may hold values from -4 to 4
- value_bias: bfloat16 [1280], P('tensor'), may hold values from -0.75 to 0.75
- out_bias: bfloat16 [1280], P(('shard', 'context')), may hold values from -4 to 4
- up_bias: bfloat16 [1280], P('tensor'), may hold values from -4 to 4
- down_bias: bfloat16 [1280], P(('shard', 'context')), may hold values from -4 to 4
Outputs:
- prompt_output: bfloat16 [8, 2048, 1280], P('shard', 'context')
- later_output: bfloat16 [8, 8, 256, 1280], P('shard', 'context')
- prompt_grad: float32 [8, 2048, 1280], P('shard', 'context')
- later_grad: float32 [8, 8, 256, 1280], P('shard', 'context')
- query_weight_grad: float32 [1280, 1280], P(('shard', 'context'), 'tensor')
- key_weight_grad: float32 [1280, 1280], P(('shard', 'context'), 'tensor')
- value_weight_grad: float32 [1280, 1280], P(('shard', 'context'), 'tensor')
- out_weight_grad: float32 [1280, 1280], P('tensor', ('shard', 'context'))
- up_weight_grad: float32 [1280, 1280], P(('shard', 'context'), 'tensor')
- down_weight_grad: float32 [1280, 1280], P('tensor', ('shard', 'context'))
- pre_gain_grad: float32 [1280], P(('shard', 'context'))
- pre_shift_grad: float32 [1280], P(('shard', 'context'))
- mid_gain_grad: float32 [1280], P(('shard', 'context'))
- mid_shift_grad: float32 [1280], P(('shard', 'context'))
- query_bias_grad: float32 [1280], P('tensor')
- value_bias_grad: float32 [1280], P('tensor')
- out_bias_grad: float32 [1280], P(('shard', 'context'))
- up_bias_grad: float32 [1280], P('tensor')
- down_bias_grad: float32 [1280], P(('shard', 'context'))
- output_magnitude: float32 [8], P('shard')
The draws below stay inside these ranges and needn't reach their ends.
Inputs may be any that keep to these rules, and one draw needn't show every extreme that they name: `prompt_tokens`: the block's input on the prompt rows. `later_tokens`: the block's input on the continuations.
All inputs are finite; a program needn't handle non-finite values.
Results may differ from the reference program's by a relative error of at most 0.019.
Values may be sent and summed in bfloat16 or wider, within the bound.
No kernel may reach another device: no remote copies, remote signals or barrier semaphores. Data moves between devices by JAX's collectives and lax.ppermute only.
A program may use at most 448 MiB of HBM per device.

```python
import jax
import jax.numpy as jnp
from jax import lax

D = 1280
HEADS = 8
HEAD = 160
FF = 1280
PROMPT = 2048
CONT = 256
NCONT = 8
GROUPS = 8
PAD_MOST = 512


def draw_prompt_tokens(key, part):
    place = (jnp.arange(PROMPT, dtype=jnp.float32) + 0.5) / PROMPT
    base = jnp.clip(jax.random.normal(key, (GROUPS, PROMPT, D), jnp.float32), -6.0, 6.0)
    ramp = 1.0 + 2.0 * place
    return (base * ramp[None, :, None]).astype(jnp.bfloat16)


def draw_later_tokens(key, part):
    place = (jnp.arange(NCONT, dtype=jnp.float32) + 0.5) / NCONT
    base = jnp.clip(jax.random.normal(key, (GROUPS, NCONT, CONT, D), jnp.float32), -6.0, 6.0)
    ramp = 1.0 + 2.0 * place
    return (base * ramp[None, :, None, None]).astype(jnp.bfloat16)


def draw_up_weight(key, part):
    spread = D ** (-0.5)
    entry_key = jax.random.fold_in(key, 11)
    column_key = jax.random.fold_in(key, 23)
    base = jnp.clip(jax.random.normal(entry_key, (D, FF), jnp.float32), -5.0, 5.0)
    column = 0.6 * jnp.clip(jax.random.normal(column_key, (1, FF), jnp.float32), -4.0, 4.0)
    return ((base + column) * spread).astype(jnp.bfloat16)


def place_ends(values, stream_key, smallest, top_value):
    longest = values.shape.index(max(values.shape))
    spots = []
    for shift in (0, 1):
        where = [jax.random.randint(jax.random.fold_in(stream_key, axis), (), 0, length) for axis, length in enumerate(values.shape)]
        where[longest] = (where[longest] + shift) % values.shape[longest]
        spots.append(tuple(where))
    return values.at[spots[0]].set(smallest).at[spots[1]].set(top_value)


def steps_of(rng, shape, split, low, largest):
    loudness = 1.0
    for position, parts in split:
        heights = jax.random.uniform(jax.random.fold_in(jax.random.fold_in(rng, 6), position), (parts,), jnp.float32, low / len(split), largest / len(split))
        loudness = loudness * jnp.repeat(jnp.exp(heights), shape[position] // parts).reshape((-1,) + (1,) * (len(shape) - 1 - position))
    return loudness


def scatter_about(key, dims, scale, bound, shards=(), kind=jnp.bfloat16):
    loudness = steps_of(key, dims, shards, -0.22, 0.18) if shards else 1.0
    values = jax.random.normal(key, dims, jnp.float32) * scale * loudness
    return jnp.minimum(jnp.maximum(values, -bound), bound).astype(kind)


def setup_inputs(seed: int = 0) -> dict:
    seeds = jax.random.split(jax.random.key(seed), 22)
    prompt_tokens = draw_prompt_tokens(jax.random.fold_in(seeds[21], 71), 0)
    later_tokens = draw_later_tokens(jax.random.fold_in(seeds[21], 71), 0)
    prompt_upstream = scatter_about(seeds[2], (GROUPS, PROMPT, D), 1.0, 6.0, ((0, 4), (1, 2)))
    later_upstream = scatter_about(seeds[3], (GROUPS, NCONT, CONT, D), 1.0, 6.0, ((0, 4), (1, 2)))
    prompt_lengths = place_ends(jax.random.randint(seeds[4], (GROUPS,), PROMPT - PAD_MOST, PROMPT + 1), jax.random.fold_in(seeds[4], 1), PROMPT - PAD_MOST, PROMPT).astype(jnp.int32)
    later_lengths = place_ends(jax.random.randint(seeds[5], (GROUPS, NCONT), CONT // 4, CONT + 1), jax.random.fold_in(seeds[5], 1), CONT // 4, CONT).astype(jnp.int32)
    query_weight = scatter_about(seeds[6], (D, D), D ** -0.5, 0.15625, ((0, 8), (1, 4)))
    key_weight = scatter_about(seeds[7], (D, D), D ** -0.5, 0.15625, ((0, 8), (1, 4)))
    value_weight = scatter_about(seeds[8], (D, D), D ** -0.5, 0.15625, ((0, 8), (1, 4)))
    out_weight = scatter_about(seeds[9], (D, D), (max(D // 160, 1)) ** -0.5, 2.0, ((0, 4), (1, 8)))
    up_weight = draw_up_weight(jax.random.fold_in(seeds[21], 71), 0)
    down_weight = scatter_about(seeds[11], (FF, D), FF ** -0.5, 0.15625, ((0, 4), (1, 8)))
    pre_gain = jnp.clip(1.0 + 0.18 * jax.random.normal(seeds[12], (D,), jnp.float32), 0.099609375, 1.8984375).astype(jnp.bfloat16)
    pre_shift = scatter_about(seeds[13], (D,), 0.3, 4.0, ((0, 8),))
    mid_gain = jnp.clip(1.0 + 0.18 * jax.random.normal(seeds[14], (D,), jnp.float32), 0.099609375, 1.8984375).astype(jnp.bfloat16)
    mid_shift = scatter_about(seeds[15], (D,), 0.3, 4.0, ((0, 8),))
    query_bias = scatter_about(seeds[16], (D,), 0.3, 4.0, ((0, 4),))
    value_bias = scatter_about(seeds[17], (D,), 0.05, 0.75, ((0, 4),))
    out_bias = scatter_about(seeds[18], (D,), 0.3, 4.0, ((0, 8),))
    up_bias = scatter_about(seeds[19], (FF,), 0.5, 4.0, ((0, 4),))
    down_bias = scatter_about(seeds[20], (D,), 0.3, 4.0, ((0, 8),))
    return dict(prompt_tokens=prompt_tokens, later_tokens=later_tokens, prompt_upstream=prompt_upstream, later_upstream=later_upstream, prompt_lengths=prompt_lengths, later_lengths=later_lengths, query_weight=query_weight, key_weight=key_weight, value_weight=value_weight, out_weight=out_weight, up_weight=up_weight, down_weight=down_weight, pre_gain=pre_gain, pre_shift=pre_shift, mid_gain=mid_gain, mid_shift=mid_shift, query_bias=query_bias, value_bias=value_bias, out_bias=out_bias, up_bias=up_bias, down_bias=down_bias)


EPSILON = 1e-05
MASKED = -1e+30
FINEST = lax.Precision.HIGHEST

@jax.custom_vjp
def low(v):
    return lax.optimization_barrier(v.astype(jnp.bfloat16)).astype(jnp.float32)

@jax.custom_vjp
def low_back(v):
    return v

def low_keep(v):
    return (low(v), None)

def low_pass(kept, grad):
    return (grad,)

def back_keep(v):
    return (v, None)

def back_low(kept, grad):
    return (low(grad),)
low.defvjp(low_keep, low_pass)
low_back.defvjp(back_keep, back_low)

def layer_norm(values, gain, shift):
    centre = values - lax.optimization_barrier(jnp.mean(values, axis=-1, keepdims=True))
    spread = lax.optimization_barrier(jnp.mean(centre * centre, axis=-1, keepdims=True))
    return centre * lax.rsqrt(spread + EPSILON) * gain + shift

def matmul(left, right):
    return jnp.dot(left, right, precision=FINEST)

def attend(queries, keys, values, allowed):
    head_size = queries.shape[-1]
    scores = low_back(jnp.einsum('rhe,khe->hrk', queries, keys, precision=FINEST) * head_size ** (-0.5))
    scores = jnp.where(allowed[None], scores, MASKED)
    probs = jax.nn.softmax(scores, axis=-1)
    return jnp.einsum('hrk,khe->rhe', low(probs), values, precision=FINEST)

def group_forward(weights, prompt_rows, later_rows, length):
    tokens = jnp.concatenate([prompt_rows, later_rows.reshape(NCONT * CONT, D)], 0)
    normed_in = low(layer_norm(tokens, weights['pre_gain'], weights['pre_shift']))
    queries = low(low_back(matmul(normed_in, weights['query'])) + weights['query_bias']).reshape(-1, HEADS, HEAD)
    keys = low(low_back(matmul(normed_in, weights['key']))).reshape(-1, HEADS, HEAD)
    values = low(low_back(matmul(normed_in, weights['value'])) + weights['value_bias']).reshape(-1, HEADS, HEAD)
    prompt_keys = keys[:PROMPT]
    prompt_values = values[:PROMPT]
    key_open = jnp.arange(PROMPT, dtype=jnp.int32) < length
    block = min(512, PROMPT)

    def prompt_block(query_block):
        return attend(query_block, prompt_keys, prompt_values, jnp.broadcast_to(key_open[None, :], (block, PROMPT)))
    prompt_out = lax.map(jax.checkpoint(prompt_block), queries[:PROMPT].reshape(PROMPT // block, block, HEADS, HEAD))
    prompt_out = prompt_out.reshape(PROMPT, D)
    causal = jnp.arange(CONT, dtype=jnp.int32)[:, None] >= jnp.arange(CONT, dtype=jnp.int32)[None, :]
    later_open = jnp.concatenate([jnp.broadcast_to(key_open[None, :], (CONT, PROMPT)), causal], 1)

    def later_block(item):
        query_block, key_block, value_block = item
        return attend(query_block, jnp.concatenate([prompt_keys, key_block], 0), jnp.concatenate([prompt_values, value_block], 0), later_open)
    later_out = lax.map(jax.checkpoint(later_block), (queries[PROMPT:].reshape(NCONT, CONT, HEADS, HEAD), keys[PROMPT:].reshape(NCONT, CONT, HEADS, HEAD), values[PROMPT:].reshape(NCONT, CONT, HEADS, HEAD)))
    later_out = later_out.reshape(NCONT * CONT, D)
    attended = low(low_back(jnp.concatenate([prompt_out, later_out], 0)))
    mixed = tokens + low_back(matmul(attended, weights['out'])) + weights['out_bias']
    normed_mid = low(layer_norm(mixed, weights['mid_gain'], weights['mid_shift']))
    upper = low_back(matmul(normed_mid, weights['up'])) + weights['up_bias']
    active = low(jax.nn.gelu(upper, approximate=False))
    output = mixed + matmul(active, weights['down']) + weights['down_bias']
    return (output[:PROMPT], output[PROMPT:].reshape(NCONT, CONT, D))

def reference(prompt_tokens, later_tokens, prompt_upstream, later_upstream, prompt_lengths, later_lengths, query_weight, key_weight, value_weight, out_weight, up_weight, down_weight, pre_gain, pre_shift, mid_gain, mid_shift, query_bias, value_bias, out_bias, up_bias, down_bias):
    weights = {'query': query_weight, 'key': key_weight, 'value': value_weight, 'out': out_weight, 'up': up_weight, 'down': down_weight, 'pre_gain': pre_gain, 'pre_shift': pre_shift, 'mid_gain': mid_gain, 'mid_shift': mid_shift, 'query_bias': query_bias, 'value_bias': value_bias, 'out_bias': out_bias, 'up_bias': up_bias, 'down_bias': down_bias}
    weights = jax.tree.map(lambda array: array.astype(jnp.float32), weights)
    prompt_float = prompt_tokens.astype(jnp.float32)
    later_float = later_tokens.astype(jnp.float32)

    def forward(layer_weights, prompt_part, later_part):

        def one_group(item):
            prompt_rows, later_rows, length = item
            return group_forward(layer_weights, prompt_rows, later_rows, length)
        return lax.map(jax.checkpoint(one_group), (prompt_part, later_part, prompt_lengths))
    outputs, pullback = jax.vjp(forward, weights, prompt_float, later_float)
    prompt_out, later_out = outputs
    prompt_valid = (jnp.arange(PROMPT, dtype=jnp.int32)[None, :] < prompt_lengths[:, None]).astype(jnp.float32)
    later_valid = (jnp.arange(CONT, dtype=jnp.int32)[None, None, :] < later_lengths[:, :, None]).astype(jnp.float32)
    grads, prompt_grad, later_grad = pullback((prompt_upstream.astype(jnp.float32) * prompt_valid[..., None], later_upstream.astype(jnp.float32) * later_valid[..., None]))
    squares = lax.optimization_barrier(jnp.sum(prompt_out * prompt_out * prompt_valid[..., None], axis=(1, 2)))
    squares = squares + lax.optimization_barrier(jnp.sum(later_out * later_out * later_valid[..., None], axis=(1, 2, 3)))
    counted = lax.optimization_barrier(jnp.sum(prompt_valid, axis=1)) + lax.optimization_barrier(jnp.sum(later_valid, axis=(1, 2)))
    magnitude = jnp.sqrt(squares / (counted * D))
    return (prompt_out.astype(jnp.bfloat16), later_out.astype(jnp.bfloat16), prompt_grad, later_grad, grads['query'], grads['key'], grads['value'], grads['out'], grads['up'], grads['down'], grads['pre_gain'], grads['pre_shift'], grads['mid_gain'], grads['mid_shift'], grads['query_bias'], grads['value_bias'], grads['out_bias'], grads['up_bias'], grads['down_bias'], magnitude)
```

```python
import functools
import math

import jax
import jax.numpy as jnp
from jax import lax
from jax.experimental import pallas as pl
from jax.experimental.pallas import tpu as pltpu
from jax.sharding import PartitionSpec as P

S, C, T = "shard", "context", "tensor"
SC = (S, C)
ALL = (S, C, T)
HEAD = 160
WIDE = 256
PAIR = 2
EPSILON = 1e-05
MASKED = -1e30
SCALE = HEAD**-0.5
LOG2E = math.log2(math.e)
VMEM = 58 * 1024 * 1024
bf16 = jnp.bfloat16
f32 = jnp.float32


def nt(a, b):
    return lax.dot_general(a, b, (((1,), (1,)), ((), ())), preferred_element_type=f32)


def nn(a, b):
    return lax.dot_general(a, b, (((1,), (0,)), ((), ())), preferred_element_type=f32)


def tn(a, b):
    return lax.dot_general(a, b, (((0,), (0,)), ((), ())), preferred_element_type=f32)


def normalise(values):
    centre = values - jnp.mean(values, axis=-1, keepdims=True)
    spread = jnp.mean(centre * centre, axis=-1, keepdims=True)
    inverse = lax.rsqrt(spread + EPSILON)
    return centre * inverse, inverse


def norm_back(grad, unit, inverse, gain):
    e = grad * gain
    inner = e - jnp.mean(e, axis=-1, keepdims=True)
    return (inner - unit * jnp.mean(e * unit, axis=-1, keepdims=True)) * inverse


def part(h):
    return slice(h * HEAD, (h + 1) * HEAD)


def wide(h):
    return slice(h * WIDE, (h + 1) * WIDE)


def tail(values, first):
    lane = lax.broadcasted_iota(jnp.int32, (values.shape[0], WIDE - HEAD), 1)
    return jnp.concatenate([values, jnp.where(lane == 0, first, 0.0)], axis=1)


def params(count=1):
    return pltpu.CompilerParams(
        vmem_limit_bytes=VMEM, dimension_semantics=("arbitrary",) * count
    )


def whole(shape):
    return pl.BlockSpec(shape, lambda j: (0,) * len(shape))


def project_kernel(fresh, later, own, info, x_ref, w_ref, g_ref, s_ref, qb_ref, vb_ref, *rest):
    q_ref, k_ref, v_ref = rest[:3]
    w_pad = rest[-1]
    j = pl.program_id(0)
    rows = x_ref.shape[0]
    prompt_all = pl.num_programs(0) * rows - later

    @pl.when(j == 0)
    def _():
        w_pad[...] = jnp.zeros_like(w_pad)
        for i in range(3 * PAIR):
            w_pad[:, i * WIDE : i * WIDE + HEAD] = w_ref[:, part(i)]

    if fresh:
        unit, _ = normalise(x_ref[...].astype(f32))
        normed = (unit * g_ref[...] + s_ref[...]).astype(bf16)
        rest[3][...] = normed
    else:
        normed = x_ref[...]

    @pl.when(j * rows < own)
    def _():
        for h in range(PAIR):
            row = tail(qb_ref[:, part(h)] * (SCALE * LOG2E), 1.0)
            product = nn(normed, w_pad[:, wide(h)])
            q_ref[:, wide(h)] = (product * (SCALE * LOG2E) + row).astype(bf16)

    place = lax.broadcasted_iota(jnp.int32, (rows, 1), 0) + (j * rows - later)
    where = place + info[1]
    where = jnp.where(where >= prompt_all, where - prompt_all, where)
    bias = jnp.where((place < 0) | (where < info[0]), 0.0, MASKED)
    lane = lax.broadcasted_iota(jnp.int32, (rows, WIDE), 1)
    mark = jnp.where(lane == HEAD, bias, 0.0)
    for h in range(PAIR):
        k_ref[:, wide(h)] = (nn(normed, w_pad[:, wide(PAIR + h)]) + mark).astype(bf16)
        row = tail(vb_ref[:, part(h)], 1.0)
        v_ref[:, wide(h)] = (nn(normed, w_pad[:, wide(2 * PAIR + h)]) + row).astype(bf16)


def project(fresh, info, x, weight, gain, shift, q_bias, v_bias, later, own):
    total, width = x.shape
    rows = min(512, later, own - later)
    last = own // rows - 1
    cols = PAIR * WIDE
    shapes = [(own, cols), (total, cols), (total, cols)] + ([(total, width)] if fresh else [])
    specs = [pl.BlockSpec((rows, cols), lambda j: (jnp.minimum(j, last), 0))]
    specs += [pl.BlockSpec((rows, s[1]), lambda j: (j, 0)) for s in shapes[1:]]
    return pl.pallas_call(
        functools.partial(project_kernel, fresh, later, own),
        grid=(total // rows,),
        in_specs=[
            pl.BlockSpec(memory_space=pltpu.SMEM),
            pl.BlockSpec((rows, width), lambda j: (j, 0)),
            whole(weight.shape),
            whole(gain.shape),
            whole(shift.shape),
            whole(q_bias.shape),
            whole(v_bias.shape),
        ],
        out_specs=specs,
        out_shape=[jax.ShapeDtypeStruct(s, bf16) for s in shapes],
        scratch_shapes=[pltpu.VMEM((width, 3 * PAIR * WIDE), bf16)],
        compiler_params=params(),
        cost_estimate=pl.CostEstimate(
            flops=6 * total * width * cols, bytes_accessed=8 * total * width, transcendentals=0
        ),
    )(info, x, weight, gain, shift, q_bias, v_bias)


def causal(count):
    row = lax.broadcasted_iota(jnp.int32, (count, count), 0)
    return row >= lax.broadcasted_iota(jnp.int32, (count, count), 1)


def attend_kernel(later, cont, q_ref, k_ref, v_ref, o_ref, log_ref):
    j = pl.program_id(0)
    rows = q_ref.shape[0]
    lanes = lax.broadcasted_iota(jnp.int32, (rows, 128), 1)

    def run(is_later):
        logs = jnp.zeros((rows, 128), f32)
        outs = []
        for h in range(PAIR):
            q = q_ref[:, wide(h)]
            scores = nt(q, k_ref[later:, wide(h)])
            top = jnp.max(scores, axis=1, keepdims=True)
            if is_later:
                near = []
                for i in range(rows // cont):
                    at = pl.ds(pl.multiple_of(j * rows + i * cont, cont), cont)
                    block = nt(q[i * cont : (i + 1) * cont], k_ref[at, wide(h)])
                    near.append(jnp.where(causal(cont), block, MASKED))
                near = jnp.concatenate(near, axis=0)
                top = jnp.maximum(top, jnp.max(near, axis=1, keepdims=True))
            out = nn(jnp.exp2(scores - top).astype(bf16), v_ref[later:, wide(h)])
            if is_later:
                near = jnp.exp2(near - top).astype(bf16)
                extra = []
                for i in range(rows // cont):
                    at = pl.ds(pl.multiple_of(j * rows + i * cont, cont), cont)
                    extra.append(nn(near[i * cont : (i + 1) * cont], v_ref[at, wide(h)]))
                out = out + jnp.concatenate(extra, axis=0)
            total = out[:, HEAD : HEAD + 1]
            outs.append(out[:, :HEAD] * (1.0 / total))
            logs = jnp.where(lanes == h, top + jnp.log2(total), logs)
        o_ref[...] = jnp.concatenate(outs, axis=1).astype(bf16)
        log_ref[...] = logs

    pl.when(j * rows < later)(lambda: run(True))
    pl.when(j * rows >= later)(lambda: run(False))


def attend(q, k, v, later, cont):
    own, cols = q.shape
    rows = min(512, later, own - later)
    block = lambda n: pl.BlockSpec((rows, n), lambda j: (j, 0))
    return pl.pallas_call(
        functools.partial(attend_kernel, later, cont),
        grid=(own // rows,),
        in_specs=[block(cols), whole(k.shape), whole(v.shape)],
        out_specs=[block(PAIR * HEAD), block(128)],
        out_shape=[
            jax.ShapeDtypeStruct((own, PAIR * HEAD), bf16),
            jax.ShapeDtypeStruct((own, 128), f32),
        ],
        compiler_params=params(),
        cost_estimate=pl.CostEstimate(
            flops=8 * own * k.shape[0] * cols // 2,
            bytes_accessed=8 * own * cols,
            transcendentals=own * k.shape[0],
        ),
    )(q, k, v)


def attend_back_kernel(
    later, cont, q_ref, k_ref, v_ref, o_ref, log_ref, g_ref, dq_ref, dk_ref, dv_ref, dk, dv
):
    j = pl.program_id(0)
    rows = q_ref.shape[0]

    @pl.when(j == 0)
    def _():
        dk[...] = jnp.zeros_like(dk)
        dv[...] = jnp.zeros_like(dv)

    def run(is_later):
        outs = []
        for h in range(PAIR):
            q = q_ref[:, wide(h)]
            log = log_ref[:, h : h + 1]
            g = g_ref[:, part(h)].astype(f32)
            inner = jnp.sum(g * o_ref[:, part(h)].astype(f32), axis=1, keepdims=True)
            g = tail(g, 0.0).astype(bf16)
            k = k_ref[later:, wide(h)]
            probs = jnp.exp2(nt(q, k) - log)
            drift = (probs * (nt(g, v_ref[later:, wide(h)]) - inner)).astype(bf16)
            dv[later:, wide(h)] += tn(probs.astype(bf16), g)
            dk[later:, wide(h)] += tn(drift, q)
            dq = nn(drift, k)
            if is_later:
                extra = []
                for i in range(rows // cont):
                    at = pl.ds(pl.multiple_of(j * rows + i * cont, cont), cont)
                    mine = slice(i * cont, (i + 1) * cont)
                    k = k_ref[at, wide(h)]
                    probs = jnp.where(causal(cont), jnp.exp2(nt(q[mine], k) - log[mine]), 0.0)
                    drift = nt(g[mine], v_ref[at, wide(h)]) - inner[mine]
                    drift = (probs * drift).astype(bf16)
                    dv[at, wide(h)] += tn(probs.astype(bf16), g[mine])
                    dk[at, wide(h)] += tn(drift, q[mine])
                    extra.append(nn(drift, k))
                dq = dq + jnp.concatenate(extra, axis=0)
            outs.append(dq[:, :HEAD] * SCALE)
        dq_ref[...] = jnp.concatenate(outs, axis=1).astype(bf16)

    pl.when(j * rows < later)(lambda: run(True))
    pl.when(j * rows >= later)(lambda: run(False))

    @pl.when(j == pl.num_programs(0) - 1)
    def _():
        outs = [dk[:, h * WIDE : h * WIDE + HEAD] * (1.0 / LOG2E) for h in range(PAIR)]
        dk_ref[...] = jnp.concatenate(outs, axis=1).astype(bf16)
        outs = [dv[:, h * WIDE : h * WIDE + HEAD] for h in range(PAIR)]
        dv_ref[...] = jnp.concatenate(outs, axis=1).astype(bf16)


def attend_back(q, k, v, out, logs, grad, later, cont):
    own, cols = q.shape
    total = k.shape[0]
    dense = PAIR * HEAD
    rows = min(512, later, own - later)
    block = lambda n: pl.BlockSpec((rows, n), lambda j: (j, 0))
    return pl.pallas_call(
        functools.partial(attend_back_kernel, later, cont),
        grid=(own // rows,),
        in_specs=[block(cols), whole(k.shape), whole(v.shape), block(dense), block(128), block(dense)],
        out_specs=[block(dense), whole((total, dense)), whole((total, dense))],
        out_shape=[
            jax.ShapeDtypeStruct((own, dense), bf16),
            jax.ShapeDtypeStruct((total, dense), bf16),
            jax.ShapeDtypeStruct((total, dense), bf16),
        ],
        scratch_shapes=[pltpu.VMEM((total, cols), f32)] * 2,
        compiler_params=params(),
        cost_estimate=pl.CostEstimate(
            flops=10 * own * total * cols,
            bytes_accessed=16 * own * cols,
            transcendentals=own * total * PAIR,
        ),
    )(q, k, v, out, logs, grad)


def swap(value, axis, bit):
    count = lax.axis_size(axis)
    return lax.ppermute(value, axis, [(i, i ^ bit) for i in range(count)])


def in_order(index, mine, theirs, axis=0):
    first = index == 0
    return jnp.stack(
        [jnp.where(first, mine, theirs), jnp.where(first, theirs, mine)], axis=axis
    )


def gather_rows(piece):
    if lax.axis_size(C) != 2:
        return lax.all_gather(piece, SC, axis=0, tiled=True)
    stacked = lax.all_gather(piece, S, axis=0, tiled=False)
    other = swap(stacked, C, 1)
    return in_order(lax.axis_index(C), stacked, other, 1).reshape(-1, piece.shape[1])


def scatter_rows(whole_sum):
    n = lax.axis_size(S) * lax.axis_size(C)
    low = whole_sum.astype(bf16)
    if lax.axis_size(C) != 2:
        return lax.psum_scatter(low, SC, scatter_dimension=0, tiled=True).astype(f32)
    split = whole_sum.reshape(lax.axis_size(S), 2, -1, whole_sum.shape[1])
    x = lax.axis_index(C)
    away = lax.dynamic_index_in_dim(split, 1 - x, 1, keepdims=False)
    keep = lax.dynamic_index_in_dim(split, x, 1, keepdims=False)
    summed = keep.astype(f32) + swap(away.astype(bf16), C, 1).astype(f32)
    summed = summed.reshape(-1, whole_sum.shape[1]).astype(bf16)
    return lax.psum_scatter(summed, S, scatter_dimension=0, tiled=True).astype(f32)


def pick(array, index, axis=0):
    return lax.dynamic_index_in_dim(array, index, axis, keepdims=False)


def body(
    prompt_tokens,
    later_tokens,
    prompt_upstream,
    later_upstream,
    prompt_lengths,
    later_lengths,
    query_weight,
    key_weight,
    value_weight,
    out_weight,
    up_weight,
    down_weight,
    pre_gain,
    pre_shift,
    mid_gain,
    mid_shift,
    query_bias,
    value_bias,
    out_bias,
    up_bias,
    down_bias,
):
    groups, prompt_rows, width = prompt_tokens.shape
    count, cont = later_tokens.shape[1:3]
    later = count * cont
    own = later + prompt_rows
    contexts = lax.axis_size(C)
    prompt_all = prompt_rows * contexts
    cols = query_weight.shape[1]
    x = lax.axis_index(C)
    t = lax.axis_index(T)
    y, c = t // 2, t % 2
    turn = (t, t ^ 2, t ^ 1, t ^ 3)

    def mine(array):
        return pick(array.reshape(2, 2, -1, *array.shape[1:]), c, 1).reshape(
            -1, *array.shape[1:]
        )

    def theirs(array):
        return pick(array.reshape(2, 2, -1, *array.shape[1:]), 1 - c, 1).reshape(
            -1, *array.shape[1:]
        )

    def join(own_half, other_half):
        a = own_half.reshape(2, -1, own_half.shape[-1])
        b = other_half.reshape(2, -1, own_half.shape[-1])
        return in_order(c, a, b, 1).reshape(-1, own_half.shape[-1])

    qkv_own = gather_rows(jnp.concatenate([query_weight, key_weight, value_weight], axis=1))
    oud_own = gather_rows(jnp.concatenate([out_weight.T, up_weight, down_weight.T], axis=1))
    vectors = jnp.stack([pre_gain, pre_shift, mid_gain, mid_shift, out_bias, down_bias])
    vectors = lax.all_gather(vectors, SC, axis=1, tiled=True).astype(f32)
    pre_gain, pre_shift, mid_gain, mid_shift, out_bias, down_bias = [
        vectors[i : i + 1] for i in range(6)
    ]
    biases = lax.all_gather(jnp.stack([query_bias, value_bias, up_bias]), T).astype(f32)
    biases = jnp.stack([pick(biases, i) for i in turn])
    up_bias = biases[:, 2].reshape(1, -1)

    prompt = pick(prompt_tokens, y)
    follow = pick(later_tokens, y).reshape(later, width)
    tokens = jnp.concatenate([follow, prompt], axis=0)
    if contexts == 2:
        half = pick(prompt.reshape(2, -1, width), c)
        half = swap(half, C, 1)
        beyond = in_order(c, half, swap(half, T, 1)).reshape(-1, width)
    else:
        beyond = lax.all_gather(prompt, C)
        beyond = jnp.roll(beyond, -x, axis=0)[1:].reshape(-1, width)
    length = pick(prompt_lengths, y)
    lengths = pick(later_lengths, y)
    info = jnp.stack([length, x * prompt_rows]).astype(jnp.int32)

    qkv_far = swap(qkv_own, T, 2)
    oud_far = swap(oud_own, T, 2)
    oud_pair = jnp.stack([oud_own, oud_far])
    oud_core = swap(oud_pair, T, 1)

    q0, k0, v0, normed_in = project(
        True,
        info,
        jnp.concatenate([tokens, beyond], axis=0),
        qkv_own,
        pre_gain,
        pre_shift,
        biases[0, 0:1],
        biases[0, 1:2],
        later,
        own,
    )
    a0, log0 = attend(q0, k0, v0, later, cont)
    q1, k1, v1 = project(
        False, info, normed_in, qkv_far, pre_gain, pre_shift,
        biases[1, 0:1], biases[1, 1:2], later, own,
    )
    a1, log1 = attend(q1, k1, v1, later, cont)

    attended = jnp.concatenate([a0, a1], axis=1)
    attended = jnp.concatenate([mine(attended), swap(theirs(attended), T, 1)], axis=1)
    out_t, up, down_t = [
        jnp.concatenate(
            [w[:, i * cols : (i + 1) * cols] for w in (oud_own, oud_far, oud_core[0], oud_core[1])],
            axis=1,
        )
        for i in range(3)
    ]
    row_tokens = mine(tokens).astype(f32)
    mixed = row_tokens + nt(attended, out_t) + out_bias
    unit, inverse = normalise(mixed)
    normed_mid = (unit * mid_gain + mid_shift).astype(bf16)
    upper = nn(normed_mid, up) + up_bias
    cumulative = 0.5 * (1.0 + lax.erf(upper * (0.5**0.5)))
    active = (upper * cumulative).astype(bf16)
    output = mixed + nt(active, down_t) + down_bias

    later_valid = jnp.arange(cont, dtype=jnp.int32)[None, :] < lengths[:, None]
    prompt_valid = x * prompt_rows + jnp.arange(prompt_rows, dtype=jnp.int32) < length
    valid = jnp.concatenate([later_valid.reshape(later), prompt_valid]).astype(f32)
    valid = mine(valid[:, None])
    squares = jnp.sum(output * output * valid)
    here = (jnp.arange(groups, dtype=jnp.int32) == y).astype(f32)[:, None]
    sums = here * jnp.stack([squares, jnp.sum(valid)])[None, :]
    sums = lax.psum(sums, (C, T))
    magnitude = jnp.sqrt(sums[:, 0] / (sums[:, 1] * width))

    output_low = output.astype(bf16)

    def spread(rows_mine):
        other = swap(rows_mine, T, 2)
        both = jnp.stack([rows_mine, other])
        core = swap(both, T, 1)
        near, far = join(both[0], core[0]), join(both[1], core[1])
        full = in_order(y, near, far)
        follow = full[:, :later].reshape(groups, count, cont, width)
        return full[:, later:], follow

    prompt_output, later_output = spread(output_low)

    upstream = jnp.concatenate(
        [pick(later_upstream, y).reshape(later, width), pick(prompt_upstream, y)], axis=0
    )
    grad_low = (mine(upstream).astype(f32) * valid).astype(bf16)
    grad_out = grad_low.astype(f32)
    down_grad = tn(grad_low, active)
    down_bias_grad = jnp.sum(grad_out, axis=0)
    density = jnp.exp(-0.5 * upper * upper) * (1.0 / math.sqrt(2.0 * math.pi))
    grad_upper = nn(grad_low, down_t) * (cumulative + upper * density)
    grad_upper_low = grad_upper.astype(bf16)
    up_grad = tn(normed_mid, grad_upper_low)
    up_bias_grad = jnp.sum(grad_upper, axis=0)
    grad_mid = nt(grad_upper_low, up)
    mid_gain_grad = jnp.sum(grad_mid * unit, axis=0)
    mid_shift_grad = jnp.sum(grad_mid, axis=0)
    grad_mixed = grad_out + norm_back(grad_mid, unit, inverse, mid_gain)
    grad_mixed_low = grad_mixed.astype(bf16)
    out_grad = tn(grad_mixed_low, attended)
    out_bias_grad = jnp.sum(grad_mixed, axis=0)
    grad_attended = nn(grad_mixed_low, out_t).astype(bf16)

    def over_cores(grad):
        grad = grad.astype(bf16).reshape(width, 4, cols)
        return grad[:, :2].reshape(width, -1), grad[:, 2:].reshape(width, -1)

    pairs = [over_cores(g) for g in (out_grad, up_grad, down_grad)]
    summed = [a.astype(f32) + swap(b, T, 1).astype(f32) for a, b in pairs]
    near = jnp.concatenate([g[:, :cols] for g in summed], axis=1)
    far = jnp.concatenate([g[:, cols:] for g in summed], axis=1)
    oud_grad = scatter_rows(near + swap(far.astype(bf16), T, 2).astype(f32))
    out_weight_grad = oud_grad[:, :cols].T
    up_weight_grad = oud_grad[:, cols : 2 * cols]
    down_weight_grad = oud_grad[:, 2 * cols :].T

    half = 2 * cols
    grad_heads = join(grad_attended[:, :half], swap(grad_attended[:, half:], T, 1))
    dq0, dk0, dv0 = attend_back(q0, k0, v0, a0, log0, grad_heads[:, :cols], later, cont)
    dq1, dk1, dv1 = attend_back(q1, k1, v1, a1, log1, grad_heads[:, cols:], later, cont)

    def weight_sums(dq, dk, dv):
        return jnp.concatenate(
            [tn(normed_in[:own], dq), tn(normed_in, dk), tn(normed_in, dv)], axis=1
        )

    near = weight_sums(dq0, dk0, dv0)
    far = weight_sums(dq1, dk1, dv1)
    qkv_grad = scatter_rows(near + swap(far.astype(bf16), T, 2).astype(f32))

    own_share = nt(
        jnp.concatenate([dq0, dk0[:own], dv0[:own]], axis=1), qkv_own
    ) + nt(jnp.concatenate([dq1, dk1[:own], dv1[:own]], axis=1), qkv_far)
    beyond_share = nt(jnp.concatenate([dk0[own:], dv0[own:]], axis=1), qkv_own[:, cols:]) + nt(
        jnp.concatenate([dk1[own:], dv1[own:]], axis=1), qkv_far[:, cols:]
    )
    grad_in = mine(own_share) + swap(theirs(own_share).astype(bf16), T, 1).astype(f32)
    if contexts == 2:
        split = beyond_share.reshape(2, -1, width)
        back = pick(split, c) + swap(pick(split, 1 - c).astype(bf16), T, 1).astype(f32)
        back = swap(back.astype(bf16), C, 1).astype(f32)
    else:
        back = beyond_share + swap(beyond_share.astype(bf16), T, 1).astype(f32)
        back = back.reshape(contexts - 1, prompt_rows, width)
        back = jnp.concatenate([jnp.zeros_like(back[:1]), back], axis=0)
        back = jnp.roll(back, x, axis=0).astype(bf16)
        back = lax.psum_scatter(back, C, scatter_dimension=0, tiled=True).astype(f32)
        back = pick(back.reshape(2, -1, width), c)
    grad_in = grad_in + jnp.concatenate([jnp.zeros((later // 2, width), f32), back], axis=0)
    unit, inverse = normalise(row_tokens)
    pre_gain_grad = jnp.sum(grad_in * unit, axis=0)
    pre_shift_grad = jnp.sum(grad_in, axis=0)
    grad_tokens = grad_mixed + norm_back(grad_in, unit, inverse, pre_gain)
    prompt_grad, later_grad = spread(grad_tokens.astype(bf16))

    def placed(pieces, places):
        rows = jnp.zeros((lax.axis_size(T), cols), f32)
        for piece, place in zip(pieces, places):
            rows = lax.dynamic_update_slice(rows, piece.reshape(1, cols), (place, 0))
        return rows.reshape(-1)

    def total(values):
        return jnp.sum(values.astype(f32), axis=0)

    sums = jnp.stack(
        [
            pre_gain_grad,
            pre_shift_grad,
            mid_gain_grad,
            mid_shift_grad,
            out_bias_grad,
            down_bias_grad,
            placed([total(dq0), total(dq1)], [t, t ^ 2]),
            placed([total(dv0), total(dv1)], [t, t ^ 2]),
            placed(list(up_bias_grad.reshape(4, cols)), turn),
        ]
    )
    sums = lax.psum(sums, ALL)
    n = lax.axis_size(S) * contexts
    z = lax.axis_index(S) * contexts + x
    full = lax.dynamic_slice(sums, (0, z * (width // n)), (6, width // n))
    heads = lax.dynamic_slice(sums, (6, t * cols), (3, cols))

    return (
        prompt_output,
        later_output,
        prompt_grad.astype(f32),
        later_grad.astype(f32),
        qkv_grad[:, :cols],
        qkv_grad[:, cols : 2 * cols],
        qkv_grad[:, 2 * cols :],
        out_weight_grad,
        up_weight_grad,
        down_weight_grad,
        full[0],
        full[1],
        full[2],
        full[3],
        heads[0],
        heads[1],
        full[4],
        heads[2],
        full[5],
        magnitude,
    )


def solution(mesh):
    rows, later, vector = P(S, C, None), P(S, C, None, None), P(SC)
    weight, turned, column = P(SC, T), P(T, SC), P(T)
    return jax.shard_map(
        body,
        mesh=mesh,
        in_specs=(rows, later, rows, later, P(S), P(S, C))
        + (weight, weight, weight, turned, weight, turned)
        + (vector,) * 4
        + (column, column, vector, column, vector),
        out_specs=(rows, later, rows, later)
        + (weight, weight, weight, turned, weight, turned)
        + (vector,) * 4
        + (column, column, vector, column, vector, P(S)),
        check_vma=False,
    )
```

```python
import functools
import math

import jax
import jax.numpy as jnp
from jax import lax
from jax.experimental import pallas as pl
from jax.experimental.pallas import tpu as pltpu
from jax.sharding import PartitionSpec as P

S, C, T = "shard", "context", "tensor"
SC = (S, C)
ALL = (S, C, T)
HEAD = 160
WIDE = 256
PAIR = 2
EPSILON = 1e-05
MASKED = -1e30
SCALE = HEAD**-0.5
LOG2E = math.log2(math.e)
VMEM = 58 * 1024 * 1024
bf16 = jnp.bfloat16
f32 = jnp.float32


def nt(a, b):
    return lax.dot_general(a, b, (((1,), (1,)), ((), ())), preferred_element_type=f32)


def nn(a, b):
    return lax.dot_general(a, b, (((1,), (0,)), ((), ())), preferred_element_type=f32)


def tn(a, b):
    return lax.dot_general(a, b, (((0,), (0,)), ((), ())), preferred_element_type=f32)


def normalise(values):
    centre = values - jnp.mean(values, axis=-1, keepdims=True)
    spread = jnp.mean(centre * centre, axis=-1, keepdims=True)
    inverse = lax.rsqrt(spread + EPSILON)
    return centre * inverse, inverse


def norm_back(grad, unit, inverse, gain):
    e = grad * gain
    inner = e - jnp.mean(e, axis=-1, keepdims=True)
    return (inner - unit * jnp.mean(e * unit, axis=-1, keepdims=True)) * inverse


def part(h):
    return slice(h * HEAD, (h + 1) * HEAD)


def wide(h):
    return slice(h * WIDE, (h + 1) * WIDE)


def tail(values, first):
    lane = lax.broadcasted_iota(jnp.int32, (values.shape[0], WIDE - HEAD), 1)
    return jnp.concatenate([values, jnp.where(lane == 0, first, 0.0)], axis=1)


def params(count=1):
    return pltpu.CompilerParams(
        vmem_limit_bytes=VMEM, dimension_semantics=("arbitrary",) * count
    )


def whole(shape):
    return pl.BlockSpec(shape, lambda j, *_: (0,) * len(shape))


def once(shape):
    return pl.BlockSpec(
        shape, lambda j, *_: (0,) * len(shape), pipeline_mode=pl.Buffered(1)
    )


def cost(flops, moved, exps=0):
    return pl.CostEstimate(flops=int(flops), bytes_accessed=int(moved), transcendentals=0)


def project_kernel(fresh, own, spans, weights, info, *refs):
    x_refs, refs = refs[: len(spans)], refs[len(spans) :]
    w_refs, refs = refs[: len(weights)], refs[len(weights) :]
    qb_ref, vb_ref, q_ref, k_ref, v_ref = refs[:5]
    w_pad, columns = refs[-2:]
    vectors = refs[6] if fresh else None
    dense = 3 * PAIR * HEAD
    j = pl.program_id(0)
    rows = k_ref.shape[0]

    @pl.when(j == 0)
    def _():
        w_pad[...] = jnp.zeros_like(w_pad)
        spot = 2
        for w_ref in w_refs:
            count, deep = w_ref.shape[:2]
            for b in range(count):
                at = pl.ds(pl.multiple_of(info[spot], 16), deep)
                spot += 1
                for i in range(3 * PAIR):
                    w_pad[at, i * WIDE : i * WIDE + HEAD] = w_ref[b, :, part(i)]
                if fresh:
                    columns[at, 0:2] = w_ref[b, :, dense : dense + 2].astype(f32)
        if fresh:
            vectors[...] = columns[...].T[:8]

    if fresh:
        n_ref = refs[5]
        for x_ref, (low, high) in zip(x_refs, spans):

            @pl.when((j >= low) & (j < high))
            def _():
                unit, _ = normalise(x_ref[...].reshape(rows, -1).astype(f32))
                n_ref[...] = (unit * vectors[0:1, :] + vectors[1:2, :]).astype(bf16)

        normed = n_ref[...]
    else:
        normed = x_refs[0][...]

    @pl.when(j * rows < own)
    def _():
        for h in range(PAIR):
            row = tail(qb_ref[:, part(h)] * (SCALE * LOG2E), 1.0)
            product = nn(normed, w_pad[:, wide(h)])
            q_ref[:, wide(h)] = (product * (SCALE * LOG2E) + row).astype(bf16)

    start = info[2 + sum(weights) + j]
    where = lax.broadcasted_iota(jnp.int32, (rows, 1), 0) + start
    bias = jnp.where((start < 0) | (where < info[1]), 0.0, MASKED)
    lane = lax.broadcasted_iota(jnp.int32, (rows, WIDE), 1)
    mark = jnp.where(lane == HEAD, bias, 0.0)
    for h in range(PAIR):
        k_ref[:, wide(h)] = (nn(normed, w_pad[:, wide(PAIR + h)]) + mark).astype(bf16)
        row = tail(vb_ref[:, part(h)], 1.0)
        v_ref[:, wide(h)] = (nn(normed, w_pad[:, wide(2 * PAIR + h)]) + row).astype(bf16)


def span_spec(shape, rows, low, count, grouped):
    inside = lambda j: jnp.clip(j - low, 0, count - 1)
    if grouped:
        return pl.BlockSpec((1, rows, shape[-1]), lambda j, info: (info[0], inside(j), 0))
    return pl.BlockSpec((rows, shape[-1]), lambda j, info: (inside(j), 0))


def project(fresh, info, sources, weights, q_bias, v_bias, rows, own, total):
    width = sources[0].shape[-1]
    last = own // rows - 1
    cols = PAIR * WIDE
    spans, specs = [], []
    for x in sources:
        low = spans[-1][1] if spans else 0
        count = x.shape[-2] // rows
        spans.append((low, low + count))
        specs.append(span_spec(x.shape, rows, low, count, x.ndim == 3))
    shapes = [(own, cols), (total, cols), (total, cols)] + ([(total, width)] if fresh else [])
    outs = [pl.BlockSpec((rows, cols), lambda j, info: (jnp.minimum(j, last), 0))]
    outs += [pl.BlockSpec((rows, s[1]), lambda j, info: (j, 0)) for s in shapes[1:]]
    outs += [whole((8, width))] if fresh else []
    flat = [q_bias, v_bias]
    return pl.pallas_call(
        functools.partial(project_kernel, fresh, own, spans, [w.shape[0] for w in weights]),
        grid_spec=pltpu.PrefetchScalarGridSpec(
            num_scalar_prefetch=1,
            grid=(total // rows,),
            in_specs=specs + [once(w.shape) for w in weights] + [whole(a.shape) for a in flat],
            out_specs=outs,
            scratch_shapes=[
                pltpu.VMEM((width, 3 * PAIR * WIDE), bf16),
                pltpu.VMEM((width, 128), f32),
            ],
        ),
        out_shape=[jax.ShapeDtypeStruct(s, bf16) for s in shapes]
        + ([jax.ShapeDtypeStruct((8, width), f32)] if fresh else []),
        compiler_params=params(),
        cost_estimate=cost(14 * total * width * cols, 8 * total * width),
    )(info, *sources, *weights, *flat)


def causal(count):
    row = lax.broadcasted_iota(jnp.int32, (count, count), 0)
    return row >= lax.broadcasted_iota(jnp.int32, (count, count), 1)


def attend_kernel(later, cont, q_ref, k_ref, v_ref, o_ref, log_ref):
    j = pl.program_id(0)
    rows = q_ref.shape[0]
    lanes = lax.broadcasted_iota(jnp.int32, (rows, 128), 1)

    def run(is_later):
        logs = jnp.zeros((rows, 128), f32)
        outs = []
        for h in range(PAIR):
            q = q_ref[:, wide(h)]
            scores = nt(q, k_ref[later:, wide(h)])
            top = jnp.max(scores, axis=1, keepdims=True)
            if is_later:
                near = []
                for i in range(rows // cont):
                    at = pl.ds(pl.multiple_of(j * rows + i * cont, cont), cont)
                    block = nt(q[i * cont : (i + 1) * cont], k_ref[at, wide(h)])
                    near.append(jnp.where(causal(cont), block, MASKED))
                near = jnp.concatenate(near, axis=0)
                top = jnp.maximum(top, jnp.max(near, axis=1, keepdims=True))
            out = nn(jnp.exp2(scores - top).astype(bf16), v_ref[later:, wide(h)])
            if is_later:
                near = jnp.exp2(near - top).astype(bf16)
                extra = []
                for i in range(rows // cont):
                    at = pl.ds(pl.multiple_of(j * rows + i * cont, cont), cont)
                    extra.append(nn(near[i * cont : (i + 1) * cont], v_ref[at, wide(h)]))
                out = out + jnp.concatenate(extra, axis=0)
            total = out[:, HEAD : HEAD + 1]
            outs.append(out[:, :HEAD] * (1.0 / total))
            logs = jnp.where(lanes == h, top + jnp.log2(total), logs)
        o_ref[...] = jnp.concatenate(outs, axis=1).astype(bf16)
        log_ref[...] = logs

    pl.when(j * rows < later)(lambda: run(True))
    pl.when(j * rows >= later)(lambda: run(False))


def attend(q, k, v, later, cont):
    own, cols = q.shape
    rows = min(512, later, own - later)
    block = lambda n: pl.BlockSpec((rows, n), lambda j: (j, 0))
    return pl.pallas_call(
        functools.partial(attend_kernel, later, cont),
        grid=(own // rows,),
        in_specs=[block(cols), whole(k.shape), whole(v.shape)],
        out_specs=[block(PAIR * HEAD), block(128)],
        out_shape=[
            jax.ShapeDtypeStruct((own, PAIR * HEAD), bf16),
            jax.ShapeDtypeStruct((own, 128), f32),
        ],
        compiler_params=params(),
        cost_estimate=cost(8 * own * k.shape[0] * cols // 2, 8 * own * cols),
    )(q, k, v)


def attend_back_kernel(
    later, cont, first, q_ref, k_ref, v_ref, o_ref, log_ref, g_ref, dq_ref, dk_ref, dv_ref, dk, dv
):
    j = pl.program_id(0)
    rows = q_ref.shape[0]

    @pl.when(j == 0)
    def _():
        dk[...] = jnp.zeros_like(dk)
        dv[...] = jnp.zeros_like(dv)

    def run(is_later):
        outs = []
        for h in range(PAIR):
            q = q_ref[:, wide(h)]
            log = log_ref[:, h : h + 1]
            g = g_ref[:, part(first + h)].astype(f32)
            inner = jnp.sum(g * o_ref[:, part(h)].astype(f32), axis=1, keepdims=True)
            g = tail(g, 0.0).astype(bf16)
            k = k_ref[later:, wide(h)]
            probs = jnp.exp2(nt(q, k) - log)
            drift = (probs * (nt(g, v_ref[later:, wide(h)]) - inner)).astype(bf16)
            dv[later:, wide(h)] += tn(probs.astype(bf16), g)
            dk[later:, wide(h)] += tn(drift, q)
            dq = nn(drift, k)
            if is_later:
                extra = []
                for i in range(rows // cont):
                    at = pl.ds(pl.multiple_of(j * rows + i * cont, cont), cont)
                    mine = slice(i * cont, (i + 1) * cont)
                    k = k_ref[at, wide(h)]
                    probs = jnp.where(causal(cont), jnp.exp2(nt(q[mine], k) - log[mine]), 0.0)
                    drift = nt(g[mine], v_ref[at, wide(h)]) - inner[mine]
                    drift = (probs * drift).astype(bf16)
                    dv[at, wide(h)] += tn(probs.astype(bf16), g[mine])
                    dk[at, wide(h)] += tn(drift, q[mine])
                    extra.append(nn(drift, k))
                dq = dq + jnp.concatenate(extra, axis=0)
            outs.append(dq[:, :HEAD] * SCALE)
        dq_ref[...] = jnp.concatenate(outs, axis=1).astype(bf16)

    pl.when(j * rows < later)(lambda: run(True))
    pl.when(j * rows >= later)(lambda: run(False))

    @pl.when(j == pl.num_programs(0) - 1)
    def _():
        outs = [dk[:, h * WIDE : h * WIDE + HEAD] * (1.0 / LOG2E) for h in range(PAIR)]
        dk_ref[...] = jnp.concatenate(outs, axis=1).astype(bf16)
        outs = [dv[:, h * WIDE : h * WIDE + HEAD] for h in range(PAIR)]
        dv_ref[...] = jnp.concatenate(outs, axis=1).astype(bf16)


def attend_back(q, k, v, out, logs, grad, first, later, cont):
    own, cols = q.shape
    total = k.shape[0]
    dense = PAIR * HEAD
    rows = min(512, later, own - later)
    block = lambda n: pl.BlockSpec((rows, n), lambda j: (j, 0))
    return pl.pallas_call(
        functools.partial(attend_back_kernel, later, cont, first),
        grid=(own // rows,),
        in_specs=[block(cols), whole(k.shape), whole(v.shape), block(dense), block(128), block(grad.shape[1])],
        out_specs=[block(dense), whole((total, dense)), whole((total, dense))],
        out_shape=[
            jax.ShapeDtypeStruct((own, dense), bf16),
            jax.ShapeDtypeStruct((total, dense), bf16),
            jax.ShapeDtypeStruct((total, dense), bf16),
        ],
        scratch_shapes=[pltpu.VMEM((total, cols), f32)] * 2,
        compiler_params=params(),
        cost_estimate=cost(1000, 1000),
    )(q, k, v, out, logs, grad)


WEIGHTS = 3


def middle_kernel(counts, info, tok_ref, go_ref, valid_ref, *refs):
    a_refs, refs = refs[:4], refs[4:]
    w_refs, refs = refs[: 4 * len(counts)], refs[4 * len(counts) :]
    ub_ref, y_ref, gm_ref, near_ref, far_ref, sum_ref, keep_ref, send_ref = refs[:8]
    w, acc, att, columns, vectors, sem = refs[8:]
    j = pl.program_id(0)
    cols = a_refs[0].shape[1]
    half = 2 * cols

    @pl.when(j == 0)
    def _():
        acc[...] = jnp.zeros_like(acc)
        sum_ref[...] = jnp.zeros_like(sum_ref)
        for r in range(4):
            spot = 1
            for w_ref in w_refs[r * len(counts) : (r + 1) * len(counts)]:
                count, deep = w_ref.shape[:2]
                for b in range(count):
                    at = pl.ds(pl.multiple_of(info[spot], 16), deep)
                    spot += 1
                    for m in range(WEIGHTS):
                        w[m, at, r * cols : (r + 1) * cols] = w_ref[
                            b, :, m * cols : (m + 1) * cols
                        ]
                    if r == 0:
                        columns[at, 0:4] = w_ref[b, :, 3 * cols : 3 * cols + 4].astype(f32)
        vectors[...] = columns[...].T[:8]

    for r in range(4):
        att[:, r * cols : (r + 1) * cols] = a_refs[r][...]
    attended = att[...]
    mixed = tok_ref[...].astype(f32) + nt(attended, w[0]) + vectors[2:3, :]
    unit, inverse = normalise(mixed)
    gain = vectors[0:1, :]
    normed = (unit * gain + vectors[1:2, :]).astype(bf16)
    upper = nn(normed, w[1]) + ub_ref[...]
    cumulative = 0.5 + 0.5 * lax.erf(upper * (0.5**0.5))
    active = (upper * cumulative).astype(bf16)
    output = mixed + nt(active, w[2]) + vectors[3:4, :]
    y_ref[...] = output.astype(bf16)
    sum_ref[0:1, :] += jnp.sum(output * output * valid_ref[...], axis=0, keepdims=True)

    go = go_ref[...]
    acc[2] += tn(go, active)
    density = jnp.exp(-0.5 * upper * upper) * (1.0 / math.sqrt(2.0 * math.pi))
    grad_upper = nn(go, w[2]) * (cumulative + upper * density)
    sum_ref[5:6, :] += jnp.sum(grad_upper, axis=0, keepdims=True)
    low = grad_upper.astype(bf16)
    acc[1] += tn(normed, low)
    grad_mid = nt(low, w[1])
    sum_ref[2:3, :] += jnp.sum(grad_mid * unit, axis=0, keepdims=True)
    sum_ref[3:4, :] += jnp.sum(grad_mid, axis=0, keepdims=True)
    grad_out = go.astype(f32)
    sum_ref[1:2, :] += jnp.sum(grad_out, axis=0, keepdims=True)
    grad_mixed = grad_out + norm_back(grad_mid, unit, inverse, gain)
    sum_ref[4:5, :] += jnp.sum(grad_mixed, axis=0, keepdims=True)
    gm_ref[...] = grad_mixed
    low = grad_mixed.astype(bf16)
    acc[0] += tn(low, attended)
    grad_attended = nn(low, w[0]).astype(bf16)
    near_ref[...] = grad_attended[:, :half]
    far_ref[...] = grad_attended[:, half:]

    @pl.when(j == pl.num_programs(0) - 1)
    def _():
        copies = []
        for m in range(WEIGHTS):
            w[m] = acc[m].astype(bf16)
            for i, out_ref in enumerate((keep_ref, send_ref)):
                source = w.at[m, :, pl.ds(i * half, half)]
                target = out_ref.at[:, pl.ds(m * half, half)]
                copies.append(pltpu.make_async_copy(source, target, sem.at[2 * m + i]))
                copies[-1].start()
        for copy in copies:
            copy.wait()


def middle(info, tokens, grad, valid, mine, theirs, weights, up_bias, rows, half):
    count, width = tokens.shape
    cols = mine[0].shape[1]
    per = half // rows
    block = lambda n: pl.BlockSpec((rows, n), lambda j, info: (j, 0))
    own = pl.BlockSpec(
        (rows, cols), lambda j, info: ((2 * (j // per) + info[0]) * per + j % per, 0)
    )
    flat = [w for group in weights for w in group]
    hbm = pl.BlockSpec(memory_space=pl.ANY)
    shape = jax.ShapeDtypeStruct
    return pl.pallas_call(
        functools.partial(middle_kernel, [w.shape[0] for w in weights[0]]),
        grid_spec=pltpu.PrefetchScalarGridSpec(
            num_scalar_prefetch=1,
            grid=(count // rows,),
            in_specs=[block(width), block(width), block(1), own, own, block(cols), block(cols)]
            + [once(w.shape) for w in flat]
            + [whole(up_bias.shape)],
            out_specs=[block(width), block(width), block(2 * cols), block(2 * cols)]
            + [whole((8, width)), hbm, hbm],
            scratch_shapes=[
                pltpu.VMEM((WEIGHTS, width, 4 * cols), bf16),
                pltpu.VMEM((WEIGHTS, width, 4 * cols), f32),
                pltpu.VMEM((rows, 4 * cols), bf16),
                pltpu.VMEM((width, 128), f32),
                pltpu.VMEM((8, width), f32),
                pltpu.SemaphoreType.DMA((2 * WEIGHTS,)),
            ],
        ),
        out_shape=[
            shape((count, width), bf16),
            shape((count, width), f32),
            shape((count, 2 * cols), bf16),
            shape((count, 2 * cols), bf16),
            shape((8, width), f32),
            shape((width, 2 * WEIGHTS * cols), bf16),
            shape((width, 2 * WEIGHTS * cols), bf16),
        ],
        compiler_params=params(),
        cost_estimate=cost(148 * count * width * cols, 30 * count * width),
    )(info, tokens, grad, valid, *mine, *theirs, *flat, up_bias)


BEYOND, THEIRS, MINE = 0, 1, 2


def project_back_kernel(sums, spans, more, adding, counts, info, *refs):
    x_ref, dq_ref, dk_ref, dv_ref = refs[:4]
    refs = refs[4:]
    w_refs, refs = refs[: len(counts)], refs[len(counts) :]
    prev_refs, refs = refs[:more], refs[more:]
    other, refs = refs[:adding], refs[adding:]
    outs, refs = refs[: len(spans)], refs[len(spans) :]
    d = refs[-1]
    j = pl.program_id(0)
    cols = dq_ref.shape[1]
    if spans:
        w = refs[-2]

        @pl.when(j == 0)
        def _():
            spot = 1
            for w_ref in w_refs:
                count, deep = w_ref.shape[:2]
                for b in range(count):
                    at = pl.ds(pl.multiple_of(info[spot], 16), deep)
                    w[at, : 3 * cols] = w_ref[b, :, : 3 * cols]
                    spot += 1
            w[:, 3 * cols :] = jnp.zeros_like(w[:, 3 * cols :])

    @pl.when(j == 0)
    def _():
        d[:, 3 * cols :] = jnp.zeros_like(d[:, 3 * cols :])

    asked = info[1 + sum(counts)]

    @pl.when(j < asked)
    def _():
        d[:, :cols] = jnp.zeros_like(dq_ref)

    @pl.when(j >= asked)
    def _():
        d[:, :cols] = dq_ref[...]

    d[:, cols : 2 * cols] = dk_ref[...]
    d[:, 2 * cols : 3 * cols] = dv_ref[...]
    all_d = d[...]
    if sums:
        dw_refs, (sum_ref, acc) = refs[:sums], refs[sums : sums + 2]

        @pl.when(j == 0)
        def _():
            acc[...] = jnp.zeros_like(acc)
            sum_ref[...] = jnp.zeros_like(sum_ref)

        acc[...] += tn(x_ref[...], all_d)
        sum_ref[0:1, :] += jnp.sum(all_d.astype(f32), axis=0, keepdims=True)

        @pl.when(j == pl.num_programs(0) - 1)
        def _():
            at = 0
            for piece in other:
                acc[:, at : at + piece.shape[1]] += piece[...].astype(f32)
                at += piece.shape[1]
            at = 0
            for dw_ref in dw_refs:
                dw_ref[...] = acc[:, at : at + dw_ref.shape[1]].astype(bf16)
                at += dw_ref.shape[1]

    if spans:
        grad = nt(all_d, w[...])
        for i, (low, high) in enumerate(spans):

            @pl.when((j >= low) & (j < high))
            def _():
                if more:
                    outs[i][...] = (grad + prev_refs[i][...].astype(f32)).astype(bf16)
                else:
                    outs[i][...] = grad.astype(bf16)


def tiled(count):
    return -(-count // 256) * 256


def project_back(
    sums, wanted, c, starts, x, dq, dk, dv, weights, previous, rows, half, own, other=()
):
    total, width = x.shape
    cols = dq.shape[1]
    sizes = ((total - own) // rows, own // 2 // rows, own // 2 // rows)
    n_beyond = sizes[0] if BEYOND in wanted else 0
    n_half = sizes[1]
    per = half // rows
    steps = sum(sizes[i] for i in wanted)
    info = jnp.stack([jnp.asarray(v, jnp.int32) for v in (c, *starts, n_beyond)])

    def row(j, info):
        i = j - n_beyond
        share = (i >= n_half).astype(jnp.int32)
        i = i - share * n_half
        side = jnp.where(share == 1, info[0], 1 - info[0])
        inner = (2 * (i // per) + side) * per + i % per
        return jnp.where(j < n_beyond, own // rows + j, inner)

    def dq_row(j, info):
        return jnp.minimum(row(jnp.maximum(j, n_beyond), info), own // rows - 1)

    x_spec = pl.BlockSpec((rows, width), lambda j, info: (row(j, info), 0))
    d_spec = pl.BlockSpec((rows, cols), lambda j, info: (row(j, info), 0))
    q_spec = pl.BlockSpec((rows, cols), lambda j, info: (dq_row(j, info), 0))
    parts, spans, low = [], [], 0
    if previous is not None:
        for i in wanted:
            n = sizes[i]
            spans.append((low, low + n))
            parts.append(
                pl.BlockSpec(
                    (rows, width),
                    functools.partial(lambda a, b, j, info: (jnp.clip(j - a, 0, b - 1), 0), low, n),
                )
            )
            low += n
    shape = jax.ShapeDtypeStruct
    out_specs = list(parts)
    out_shape = [shape((sizes[i] * rows, width), bf16) for i in wanted[: len(parts)]]
    scratch = []
    lanes = tiled(3 * cols)
    if sums:
        out_specs += [whole((width, n)) for n in sums] + [whole((8, lanes))]
        out_shape += [shape((width, n), bf16) for n in sums] + [shape((8, lanes), f32)]
        scratch.append(pltpu.VMEM((width, lanes), f32))
    if parts:
        scratch.append(pltpu.VMEM((width, lanes), bf16))
    scratch.append(pltpu.VMEM((rows, lanes), bf16))
    return pl.pallas_call(
        functools.partial(
            project_back_kernel,
            len(sums),
            spans,
            len(previous or []),
            len(other),
            [w.shape[0] for w in weights],
        ),
        grid_spec=pltpu.PrefetchScalarGridSpec(
            num_scalar_prefetch=1,
            grid=(steps,),
            in_specs=[x_spec, q_spec, d_spec, d_spec]
            + [once(w.shape) for w in weights]
            + (parts if previous else [])
            + [once(o.shape) for o in other],
            out_specs=out_specs,
            scratch_shapes=scratch,
        ),
        out_shape=out_shape,
        compiler_params=params(),
        cost_estimate=cost(1000, 1000),
    )(info, x, dq, dk, dv, *weights, *(previous or []), *other)


def finish_kernel(n, gain_ref, tok_ref, mix_ref, *refs):
    shares, (low_ref, sum_ref) = refs[:n], refs[n:]

    @pl.when(pl.program_id(0) == 0)
    def _():
        sum_ref[...] = jnp.zeros_like(sum_ref)

    grad = shares[0][...].astype(f32)
    for share in shares[1:]:
        grad = grad + share[...].astype(f32)
    unit, inverse = normalise(tok_ref[...].astype(f32))
    back = norm_back(grad, unit, inverse, gain_ref[0:1, :])
    low_ref[...] = (mix_ref[...] + back).astype(bf16)
    sum_ref[0:1, :] += jnp.sum(grad * unit, axis=0, keepdims=True)
    sum_ref[1:2, :] += jnp.sum(grad, axis=0, keepdims=True)


def finish(kind, gain, tokens, mixed, shares, back, half):
    width = tokens.shape[1]
    rows = min(128, half)
    n = half // rows
    block = pl.BlockSpec((rows, width), lambda j: (kind * n + j, 0))
    plain = pl.BlockSpec((rows, width), lambda j: (j, 0))
    return pl.pallas_call(
        functools.partial(finish_kernel, len(shares) + len(back)),
        grid=(n,),
        in_specs=[whole(gain.shape), block, block] + [block] * len(shares) + [plain] * len(back),
        out_specs=[plain, whole((8, width))],
        out_shape=[
            jax.ShapeDtypeStruct((half, width), bf16),
            jax.ShapeDtypeStruct((8, width), f32),
        ],
        compiler_params=params(),
        cost_estimate=cost(1000, 1000),
    )(gain, tokens, mixed, *shares, *back)


def assemble_kernel(info, *refs):
    i = pl.program_id(0)
    for m in range(4):

        @pl.when(i == m)
        def _():
            refs[4][...] = refs[m][...].astype(refs[4].dtype)[None]


def assemble(info, pieces, kind, half, dtype):
    width = pieces[0].shape[1]
    rows = half
    n = half // rows

    def source(m, i, s):
        return kind * n + jnp.where(i < m, 0, jnp.where(i > m, n - 1, s))

    def target(i, s, info):
        return info[0] ^ (i // 2), (info[1] ^ (i % 2)) * n + s, 0

    return pl.pallas_call(
        assemble_kernel,
        grid_spec=pltpu.PrefetchScalarGridSpec(
            num_scalar_prefetch=1,
            grid=(4, n),
            in_specs=[
                pl.BlockSpec(
                    (rows, width), functools.partial(lambda m, i, s, info: (source(m, i, s), 0), m)
                )
                for m in range(4)
            ],
            out_specs=pl.BlockSpec((1, rows, width), target),
        ),
        out_shape=jax.ShapeDtypeStruct((2, 2 * half, width), dtype),
        compiler_params=params(2),
        cost_estimate=cost(1000, 1000),
    )(info, *pieces)


def swap(value, axis, bit):
    count = lax.axis_size(axis)
    return lax.ppermute(value, axis, [(i, i ^ bit) for i in range(count)])


def pick(array, index, axis=0):
    return lax.dynamic_index_in_dim(array, index, axis, keepdims=False)


def in_order(index, mine, theirs, axis=0):
    first = index == 0
    return jnp.stack(
        [jnp.where(first, mine, theirs), jnp.where(first, theirs, mine)], axis=axis
    )


def direct():
    return lax.axis_size(C) == 2 and lax.axis_size(S) == 4


def phase(*values):
    return lax.optimization_barrier(values)


def over_z(piece):
    return [swap(piece, S, i) for i in (1, 2, 3)]


def z_parts(rows, axis):
    z = lax.axis_index(S)
    low = rows.astype(bf16)
    return [pick(low, z ^ i, axis) for i in (1, 2, 3)], pick(rows, z, axis)


def z_sum(mine, parts):
    for piece in parts:
        mine = mine + piece.astype(f32)
    return mine


def z_moves(parts):
    return [swap(piece, S, i + 1) for i, piece in enumerate(parts)]


def x_parts(rows, axis):
    x = lax.axis_index(C)
    shape = rows.shape
    split = rows.reshape(*shape[:axis], 4, 2, shape[axis] // 8, *shape[axis + 1 :])
    return pick(split, 1 - x, axis + 1).astype(bf16), pick(split, x, axis + 1)


def sum_over(values, axis):
    count, bit = lax.axis_size(axis), 1
    while bit < count:
        values = values + swap(values, axis, bit)
        bit *= 2
    return values


def body(
    prompt_tokens,
    later_tokens,
    prompt_upstream,
    later_upstream,
    prompt_lengths,
    later_lengths,
    query_weight,
    key_weight,
    value_weight,
    out_weight,
    up_weight,
    down_weight,
    pre_gain,
    pre_shift,
    mid_gain,
    mid_shift,
    query_bias,
    value_bias,
    out_bias,
    up_bias,
    down_bias,
):
    groups, prompt_rows, width = prompt_tokens.shape
    count, cont = later_tokens.shape[1:3]
    later = count * cont
    own = later + prompt_rows
    contexts = lax.axis_size(C)
    total = later + prompt_rows * contexts
    cols = query_weight.shape[1]
    half = later // 2
    big = min(512, later)
    x = lax.axis_index(C)
    t = lax.axis_index(T)
    y, c = t // 2, t % 2
    turn = (t, t ^ 2, t ^ 1, t ^ 3)

    def share(array, side):
        rows = array.reshape(2, 2, half, array.shape[-1])
        return pick(rows, side, 1).reshape(2 * half, array.shape[-1])

    prompt = pick(prompt_tokens, y)
    qkv_piece = jnp.concatenate(
        [query_weight, key_weight, value_weight, pre_gain[:, None], pre_shift[:, None]], axis=1
    )
    oud_piece = jnp.concatenate(
        [out_weight.T, up_weight, down_weight.T]
        + [v[:, None] for v in (mid_gain, mid_shift, out_bias, down_bias)],
        axis=1,
    )
    length = pick(prompt_lengths, y)
    lengths = pick(later_lengths, y)
    follow = pick(later_tokens, y).reshape(later, width)
    row_tokens = share(jnp.concatenate([follow, prompt], axis=0), c)
    later_valid = jnp.arange(cont, dtype=jnp.int32)[None, :] < lengths[:, None]
    prompt_valid = x * prompt_rows + jnp.arange(prompt_rows, dtype=jnp.int32) < length
    valid = jnp.concatenate([later_valid.reshape(later), prompt_valid]).astype(f32)
    valid = share(valid[:, None], c)
    upstream = jnp.concatenate(
        [pick(later_upstream, y).reshape(later, width), pick(prompt_upstream, y)], axis=0
    )
    grad_low = (share(upstream, c).astype(f32) * valid).astype(bf16)

    biases = jnp.concatenate([query_bias, value_bias, up_bias])[None]
    if direct():
        z = lax.axis_index(S)
        deep = query_weight.shape[0]
        starts = [((z ^ i) * 2 + (x ^ k)) * deep for k in (0, 1) for i in range(4)]
        places = [(1 - x) * prompt_rows + side * half for side in (c, 1 - c)]
        tokens_piece = pick(prompt.reshape(2, half, width), c)
        tokens_piece, qkv_piece = phase(tokens_piece, qkv_piece)
        tokens_piece = swap(tokens_piece, C, 1)
        parts = over_z(qkv_piece)
        rows = jnp.pad(biases, ((0, 15), (0, qkv_piece.shape[1] - biases.shape[1])))
        far_piece = swap(jnp.concatenate([qkv_piece, rows]), T, 2)
        far_piece, tokens_piece, oud_piece, row_tokens, grad_low, valid, *parts = phase(
            far_piece, tokens_piece, oud_piece, row_tokens, grad_low, valid, *parts
        )
        far_biases = far_piece[deep : deep + 1, : biases.shape[1]]
        far_piece = far_piece[:deep]
        near = jnp.stack([qkv_piece, *parts])
        qkv_own = [near, swap(near, C, 1)]
        beyond = [tokens_piece, swap(tokens_piece, T, 1)]
        parts = [far_piece, *over_z(far_piece)]
        parts = phase(*qkv_own, *beyond, *parts, oud_piece)
        qkv_own, beyond, oud_piece = list(parts[:2]), list(parts[2:4]), parts[8]
        near = jnp.stack(parts[4:8])
        qkv_far = [near, swap(near, C, 1)]
        oud_parts = over_z(oud_piece)
    else:
        starts = [0]
        rolled = jnp.roll(lax.all_gather(prompt, C), -x, axis=0)[1:]
        beyond = [rolled.reshape(-1, width)]
        places = [((x + i) % contexts) * prompt_rows for i in range(1, contexts)]
        qkv_own = [lax.all_gather(qkv_piece, SC, axis=0, tiled=True)[None]]
        qkv_far = [swap(w, T, 2) for w in qkv_own]
        far_biases = swap(biases, T, 2)
    biases = jnp.concatenate([biases, far_biases]).astype(f32)

    def ints(*values):
        return jnp.stack([jnp.asarray(v, jnp.int32) for v in values])

    blocks = [-1] * (later // big)
    blocks += [x * prompt_rows + i * big for i in range(prompt_rows // big)]
    blocks += [p + i * big for p in places for i in range(max(half if direct() else prompt_rows, big) // big)]
    info = ints(y, length, *starts, *blocks)

    q0, k0, v0, normed_in, pre_vectors = project(
        True,
        info,
        [later_tokens.reshape(groups, later, width), prompt_tokens] + beyond,
        qkv_own,
        biases[0:1, :cols],
        biases[0:1, cols : 2 * cols],
        big,
        own,
        total,
    )
    if direct():
        q0, k0, v0, normed_in, *parts = phase(q0, k0, v0, normed_in, *qkv_far, *oud_parts)
        qkv_far = parts[:2]
        near = jnp.stack([oud_piece, *parts[2:]])
        oud_own = [near, swap(near, C, 1)]
        near = swap(near, T, 2)
    a0, log0 = attend(q0, k0, v0, later, cont)
    if direct():
        a0, near, *oud_own = phase(a0, near, *oud_own)
        oud_far = [near, swap(near, C, 1)]
    else:
        oud_own = [lax.all_gather(oud_piece, SC, axis=0, tiled=True)[None]]
        oud_far = [swap(w, T, 2) for w in oud_own]
    oud = [oud_own, oud_far] + [[swap(w, T, 1) for w in ws] for ws in (oud_own, oud_far)]
    r0 = swap(share(a0, 1 - c), T, 1)
    up_bias = biases[:, 2 * cols :]
    up_bias = jnp.concatenate([up_bias, swap(up_bias, T, 1)]).reshape(1, -1)
    q1, k1, v1 = project(
        False,
        info,
        [normed_in],
        qkv_far,
        biases[1:2, :cols],
        biases[1:2, cols : 2 * cols],
        big,
        own,
        total,
    )
    if direct():
        q1, k1, v1, oud[2][0], oud[2][1], oud[3][0], r0, up_bias = phase(
            q1, k1, v1, oud[2][0], oud[2][1], oud[3][0], r0, up_bias
        )
    a1, log1 = attend(q1, k1, v1, later, cont)
    if direct():
        a1, oud_far[1] = phase(a1, oud_far[1])
        oud[3][1] = swap(oud_far[1], T, 1)
    r1 = swap(share(a1, 1 - c), T, 1)

    output, grad_mixed, grad_near, grad_away, sums, oud_keep, oud_send = middle(
        ints(c, *starts),
        row_tokens,
        grad_low,
        valid,
        [a0, a1],
        [r0, r1],
        oud,
        up_bias,
        min(256, half),
        half,
    )

    where = ints(y, c)

    outputs = [output, swap(output, T, 1), swap(output, T, 2), None]

    received = swap(grad_away, T, 1)
    grad_heads = in_order(
        c, grad_near.reshape(2, half, -1), received.reshape(2, half, -1), 1
    ).reshape(own, -1)
    oud_send = swap(oud_send, T, 1)
    wide_part = min(1024, oud_send.shape[1])
    oud_pieces = [slice(0, wide_part), slice(wide_part, None)]
    oud_pieces = [oud_keep[:, p].astype(f32) + oud_send[:, p].astype(f32) for p in oud_pieces]
    if direct():
        away, kept = zip(*[x_parts(p, 0) for p in oud_pieces])
        grad_heads, *parts = phase(grad_heads, *away, *[k.astype(bf16) for k in kept])
        away, kept = parts[:2], parts[2:]
        away[0] = swap(away[0], C, 1)
    dq, dk, dv = attend_back(q1, k1, v1, a1, log1, grad_heads, PAIR, later, cont)
    if direct():
        dq, away[0], away[1] = phase(dq, away[0], away[1])
        away[1] = swap(away[1], C, 1)
        parts, first_sum = z_parts(kept[0].astype(f32) + away[0].astype(f32), 0)
        dq, first_sum, *parts = phase(dq, first_sum, *parts)
        first_parts = z_moves(parts)
    back_rows = min(512, half)
    everything = (BEYOND, THEIRS, MINE)
    lanes = tiled(3 * cols)
    far_widths = (3 * lanes // 4, lanes // 4)
    *shares, far, far_rest, sums1 = project_back(
        far_widths, everything, c, starts, normed_in, dq, dk, dv, qkv_far, [], back_rows, half, own
    )
    if direct():
        far, far_rest, grad_heads, outputs[1], outputs[2], away[1], first_sum, *parts = phase(
            far, far_rest, grad_heads, outputs[1], outputs[2], away[1], first_sum, *first_parts
        )
        first_sum = z_sum(first_sum, parts)
        parts, last_sum = z_parts(kept[1].astype(f32) + away[1].astype(f32), 0)
        first_sum, last_sum, grad_heads, far, *parts = phase(
            first_sum, last_sum, grad_heads, far, *parts
        )
        last_parts = z_moves(parts)
    far = swap(far, T, 2)
    outputs[3] = swap(outputs[2], T, 1)
    dq, dk, dv = attend_back(q0, k0, v0, a0, log0, grad_heads, 0, later, cont)
    def near_back(sums, wanted, dq, *rest):
        previous, other = rest[0], rest[1:]
        return project_back(
            sums,
            wanted,
            c,
            starts,
            normed_in,
            dq,
            dk,
            dv,
            qkv_own,
            previous,
            back_rows,
            half,
            own,
            other,
        )

    if direct():
        dq, dk, dv, outputs[3], far, far_rest, last_sum, *parts = phase(
            dq, dk, dv, outputs[3], far, far_rest, last_sum, *last_parts
        )
        oud_grad = jnp.concatenate([first_sum, z_sum(last_sum, parts)], axis=1).astype(bf16)
        far_rest = swap(far_rest, T, 2)
        their_share, my_share = near_back((), (THEIRS, MINE), dq, shares[1:])
        their_share, my_share, dq, far_rest = phase(their_share, my_share, dq, far_rest)
        their_share = swap(their_share, T, 1)
        (beyond_share,) = near_back((), (BEYOND,), dq, shares[:1])
        shares = [my_share, their_share]
        back = [beyond_share[:half], swap(beyond_share[half:], T, 1)]
        low, sums_later = finish(0, pre_vectors, row_tokens, grad_mixed, shares, [], half)
        low, dq, sums_later, *parts = phase(low, dq, sums_later, *shares, *back)
        shares = parts[:2]
        back = swap((parts[2].astype(f32) + parts[3].astype(f32)).astype(bf16), C, 1)
        pieces = [low, None, swap(low, T, 2), None]
        *near, sums0 = near_back((lanes // 2,) * 2, everything, dq, None, far, far_rest)
        near = [n.reshape(4, 2 * deep, lanes // 2) for n in near]
        parts = [pick(n, z ^ i) for n in near for i in (1, 2, 3)]
        near = [pick(n, z) for n in near]
        near[0], near[1], sums0, *parts = phase(*near, sums0, *parts)
        early, parts = z_moves(parts[:3]), parts[3:]
        back, pieces[2] = phase(back, pieces[2])
        pieces[3] = swap(pieces[2], T, 1)
        low, sums_prompt = finish(1, pre_vectors, row_tokens, grad_mixed, shares, [back], half)
    else:
        beyond_share, their_share, my_share, near, sums0 = near_back(
            (lanes,), everything, dq, shares, far, swap(far_rest, T, 2)
        )
        shares = [my_share, swap(their_share, T, 1)]
        back = beyond_share.astype(f32) + swap(beyond_share, T, 1).astype(f32)
        back = back.reshape(contexts - 1, prompt_rows, width)
        back = jnp.concatenate([jnp.zeros_like(back[:1]), back], axis=0)
        back = jnp.roll(back, x, axis=0).astype(bf16)
        back = lax.psum_scatter(back, C, scatter_dimension=0, tiled=True)
        back = pick(back.reshape(2, half, width), c)
        low, sums_later = finish(0, pre_vectors, row_tokens, grad_mixed, shares, [], half)
        pieces = [low, swap(low, T, 1), swap(low, T, 2), None]
        low, sums_prompt = finish(1, pre_vectors, row_tokens, grad_mixed, shares, [back], half)
        oud_grad = jnp.concatenate([p.astype(bf16) for p in oud_pieces], axis=1)
        qkv_grad, oud_grad = [
            lax.psum_scatter(g, SC, scatter_dimension=0, tiled=True) for g in (near, oud_grad)
        ]
        qkv_grad = qkv_grad.astype(f32)

    def placed(*pieces):
        block = lax.broadcasted_iota(jnp.int32, (lax.axis_size(T), cols), 0)
        return sum(jnp.where(block == i, v[None], 0.0) for i, v in zip(turn, pieces)).reshape(-1)

    row = lax.broadcasted_iota(jnp.int32, (8, width), 0)
    lane = lax.broadcasted_iota(jnp.int32, (8, width), 1)
    group = lax.axis_index(S) * groups + y
    every = lax.axis_size(S) * groups
    scalars = jnp.where(lane == group, jnp.sum(sums[0]), 0.0)
    scalars = jnp.where(lane == every + group, jnp.sum(valid), scalars)
    up_sums = placed(*sums[5].reshape(4, cols))
    sums = jnp.where(row == 6, scalars, jnp.where(row == 7, up_sums[None], sums))
    q_sums = placed(sums0[0, :cols], sums1[0, :cols])
    v_sums = placed(sums0[0, 2 * cols : 3 * cols], sums1[0, 2 * cols : 3 * cols])
    more = jnp.where(row == 2, q_sums[None], jnp.where(row == 3, v_sums[None], sums_later))
    if direct():
        low, sums_prompt, sums, more, pieces[3], *rest = phase(
            low, sums_prompt, sums, more, pieces[3], *early, *parts
        )
        near[0], parts = z_sum(near[0].astype(f32), rest[:3]), z_moves(rest[3:])
    sums = jnp.concatenate([sums, more + sums_prompt])
    last = [low, None, swap(low, T, 2), None]
    pieces[1] = swap(pieces[0], T, 1)
    if not direct():
        pieces[3] = swap(pieces[2], T, 1)
    later_grad = assemble(where, pieces, 0, half, f32)
    later_output = assemble(where, outputs, 0, half, bf16)
    prompt_output = assemble(where, outputs, 1, half, bf16)
    if direct():
        later_grad, later_output, prompt_output, near[0], near[1], sums, last[2], *parts = phase(
            later_grad, later_output, prompt_output, *near, sums, last[2], *parts
        )
        near[1] = z_sum(near[1].astype(f32), parts)
        split = jnp.concatenate(near, axis=1).reshape(2, deep, lanes)
        away = swap(pick(split, 1 - x).astype(bf16), C, 1)
        qkv_grad = pick(split, x) + away.astype(f32)
    last[1] = swap(last[0], T, 1)
    last[3] = swap(last[2], T, 1)
    sums = sum_over(sum_over(sum_over(sums, C), S), T)
    squares = lax.dynamic_slice(sums[6], (lax.axis_index(S) * groups,), (groups,))
    counted = lax.dynamic_slice(sums[6], (every + lax.axis_index(S) * groups,), (groups,))
    magnitude = jnp.sqrt(squares / (counted * width))
    oud_grad = oud_grad.reshape(-1, WEIGHTS, 2, cols)
    oud_grad = oud_grad[:, :, 0].astype(f32) + swap(oud_grad[:, :, 1], T, 2).astype(f32)
    prompt_grad = assemble(where, last, 0, half, f32)
    n = width // (lax.axis_size(S) * contexts)
    place = lax.axis_index(S) * contexts + x

    def own_vector(row):
        return lax.dynamic_slice(row, (place * n,), (n,))

    def own_heads(row):
        return lax.dynamic_slice(row, (t * cols,), (cols,))

    shaped = (groups, count, cont, width)
    return (
        prompt_output,
        later_output.reshape(shaped),
        prompt_grad,
        later_grad.reshape(shaped),
        qkv_grad[:, :cols],
        qkv_grad[:, cols : 2 * cols],
        qkv_grad[:, 2 * cols : 3 * cols],
        oud_grad[:, 0].T,
        oud_grad[:, 1],
        oud_grad[:, 2].T,
        own_vector(sums[8]),
        own_vector(sums[9]),
        own_vector(sums[2]),
        own_vector(sums[3]),
        own_heads(sums[10]),
        own_heads(sums[11]),
        own_vector(sums[4]),
        own_heads(sums[7]),
        own_vector(sums[1]),
        magnitude,
    )


def solution(mesh):
    rows, later, vector = P(S, C, None), P(S, C, None, None), P(SC)
    weight, turned, column = P(SC, T), P(T, SC), P(T)
    return jax.shard_map(
        body,
        mesh=mesh,
        in_specs=(rows, later, rows, later, P(S), P(S, C))
        + (weight, weight, weight, turned, weight, turned)
        + (vector,) * 4
        + (column, column, vector, column, vector),
        out_specs=(rows, later, rows, later)
        + (weight, weight, weight, turned, weight, turned)
        + (vector,) * 4
        + (column, column, vector, column, vector, P(S)),
        check_vma=False,
    )
```

```python
import functools
import math

import jax
import jax.numpy as jnp
from jax import lax
from jax.experimental import pallas as pl
from jax.experimental.pallas import tpu as pltpu
from jax.sharding import PartitionSpec as P

S, C, T = "shard", "context", "tensor"
SC = (S, C)
ALL = (S, C, T)
HEAD = 160
WIDE = 256
PAIR = 2
EPSILON = 1e-05
MASKED = -1e30
SCALE = HEAD**-0.5
LOG2E = math.log2(math.e)
VMEM = 58 * 1024 * 1024
bf16 = jnp.bfloat16
f32 = jnp.float32


def nt(a, b):
    return lax.dot_general(a, b, (((1,), (1,)), ((), ())), preferred_element_type=f32)


def nn(a, b):
    return lax.dot_general(a, b, (((1,), (0,)), ((), ())), preferred_element_type=f32)


def tn(a, b):
    return lax.dot_general(a, b, (((0,), (0,)), ((), ())), preferred_element_type=f32)


def normalise(values):
    centre = values - jnp.mean(values, axis=-1, keepdims=True)
    spread = jnp.mean(centre * centre, axis=-1, keepdims=True)
    inverse = lax.rsqrt(spread + EPSILON)
    return centre * inverse, inverse


def norm_back(grad, unit, inverse, gain):
    e = grad * gain
    inner = e - jnp.mean(e, axis=-1, keepdims=True)
    return (inner - unit * jnp.mean(e * unit, axis=-1, keepdims=True)) * inverse


def part(h):
    return slice(h * HEAD, (h + 1) * HEAD)


def wide(h):
    return slice(h * WIDE, (h + 1) * WIDE)


def tail(values, first):
    lane = lax.broadcasted_iota(jnp.int32, (values.shape[0], WIDE - HEAD), 1)
    return jnp.concatenate([values, jnp.where(lane == 0, first, 0.0)], axis=1)


def params(count=1):
    return pltpu.CompilerParams(
        vmem_limit_bytes=VMEM, dimension_semantics=("arbitrary",) * count
    )


def whole(shape):
    return pl.BlockSpec(shape, lambda j, *_: (0,) * len(shape))


def once(shape):
    return pl.BlockSpec(
        shape, lambda j, *_: (0,) * len(shape), pipeline_mode=pl.Buffered(1)
    )


def cost(flops, moved, exps=0):
    return pl.CostEstimate(flops=int(flops), bytes_accessed=int(moved), transcendentals=0)


def project_kernel(fresh, own, spans, weights, info, *refs):
    x_refs, refs = refs[: len(spans)], refs[len(spans) :]
    w_refs, refs = refs[: len(weights)], refs[len(weights) :]
    qb_ref, vb_ref, q_ref, k_ref, v_ref = refs[:5]
    w_pad, columns = refs[-2:]
    vectors = refs[6] if fresh else None
    dense = 3 * PAIR * HEAD
    j = pl.program_id(0)
    rows = k_ref.shape[0]

    @pl.when(j == 0)
    def _():
        w_pad[...] = jnp.zeros_like(w_pad)
        spot = 2
        for w_ref in w_refs:
            count, deep = w_ref.shape[:2]
            for b in range(count):
                at = pl.ds(pl.multiple_of(info[spot], 16), deep)
                spot += 1
                for i in range(3 * PAIR):
                    w_pad[at, i * WIDE : i * WIDE + HEAD] = w_ref[b, :, part(i)]
                if fresh:
                    columns[at, 0:2] = w_ref[b, :, dense : dense + 2].astype(f32)
        if fresh:
            vectors[...] = columns[...].T[:8]

    if fresh:
        n_ref = refs[5]
        for x_ref, (low, high) in zip(x_refs, spans):

            @pl.when((j >= low) & (j < high))
            def _():
                unit, _ = normalise(x_ref[...].reshape(rows, -1).astype(f32))
                n_ref[...] = (unit * vectors[0:1, :] + vectors[1:2, :]).astype(bf16)

        normed = n_ref[...]
    else:
        normed = x_refs[0][...]

    @pl.when(j * rows < own)
    def _():
        for h in range(PAIR):
            row = tail(qb_ref[:, part(h)] * (SCALE * LOG2E), 1.0)
            product = nn(normed, w_pad[:, wide(h)])
            q_ref[:, wide(h)] = (product * (SCALE * LOG2E) + row).astype(bf16)

    start = info[2 + sum(weights) + j]
    where = lax.broadcasted_iota(jnp.int32, (rows, 1), 0) + start
    bias = jnp.where((start < 0) | (where < info[1]), 0.0, MASKED)
    lane = lax.broadcasted_iota(jnp.int32, (rows, WIDE), 1)
    mark = jnp.where(lane == HEAD, bias, 0.0)
    for h in range(PAIR):
        k_ref[:, wide(h)] = (nn(normed, w_pad[:, wide(PAIR + h)]) + mark).astype(bf16)
        row = tail(vb_ref[:, part(h)], 1.0)
        v_ref[:, wide(h)] = (nn(normed, w_pad[:, wide(2 * PAIR + h)]) + row).astype(bf16)


def span_spec(shape, rows, low, count, grouped):
    inside = lambda j: jnp.clip(j - low, 0, count - 1)
    if grouped:
        return pl.BlockSpec((1, rows, shape[-1]), lambda j, info: (info[0], inside(j), 0))
    return pl.BlockSpec((rows, shape[-1]), lambda j, info: (inside(j), 0))


def project(fresh, info, sources, weights, q_bias, v_bias, rows, own, total):
    width = sources[0].shape[-1]
    last = own // rows - 1
    cols = PAIR * WIDE
    spans, specs = [], []
    for x in sources:
        low = spans[-1][1] if spans else 0
        count = x.shape[-2] // rows
        spans.append((low, low + count))
        specs.append(span_spec(x.shape, rows, low, count, x.ndim == 3))
    shapes = [(own, cols), (total, cols), (total, cols)] + ([(total, width)] if fresh else [])
    outs = [pl.BlockSpec((rows, cols), lambda j, info: (jnp.minimum(j, last), 0))]
    outs += [pl.BlockSpec((rows, s[1]), lambda j, info: (j, 0)) for s in shapes[1:]]
    outs += [whole((8, width))] if fresh else []
    flat = [q_bias, v_bias]
    return pl.pallas_call(
        functools.partial(project_kernel, fresh, own, spans, [w.shape[0] for w in weights]),
        grid_spec=pltpu.PrefetchScalarGridSpec(
            num_scalar_prefetch=1,
            grid=(total // rows,),
            in_specs=specs + [once(w.shape) for w in weights] + [whole(a.shape) for a in flat],
            out_specs=outs,
            scratch_shapes=[
                pltpu.VMEM((width, 3 * PAIR * WIDE), bf16),
                pltpu.VMEM((width, 128), f32),
            ],
        ),
        out_shape=[jax.ShapeDtypeStruct(s, bf16) for s in shapes]
        + ([jax.ShapeDtypeStruct((8, width), f32)] if fresh else []),
        compiler_params=params(),
        cost_estimate=cost(14 * total * width * cols, 8 * total * width),
    )(info, *sources, *weights, *flat)


def causal(count):
    row = lax.broadcasted_iota(jnp.int32, (count, count), 0)
    return row >= lax.broadcasted_iota(jnp.int32, (count, count), 1)


def attend_kernel(later, cont, q_ref, k_ref, v_ref, o_ref, log_ref):
    j = pl.program_id(0)
    rows = q_ref.shape[0]
    lanes = lax.broadcasted_iota(jnp.int32, (rows, 128), 1)

    def run(is_later):
        logs = jnp.zeros((rows, 128), f32)
        outs = []
        for h in range(PAIR):
            q = q_ref[:, wide(h)]
            scores = nt(q, k_ref[later:, wide(h)])
            top = jnp.max(scores, axis=1, keepdims=True)
            if is_later:
                near = []
                for i in range(rows // cont):
                    at = pl.ds(pl.multiple_of(j * rows + i * cont, cont), cont)
                    block = nt(q[i * cont : (i + 1) * cont], k_ref[at, wide(h)])
                    near.append(jnp.where(causal(cont), block, MASKED))
                near = jnp.concatenate(near, axis=0)
                top = jnp.maximum(top, jnp.max(near, axis=1, keepdims=True))
            out = nn(jnp.exp2(scores - top).astype(bf16), v_ref[later:, wide(h)])
            if is_later:
                near = jnp.exp2(near - top).astype(bf16)
                extra = []
                for i in range(rows // cont):
                    at = pl.ds(pl.multiple_of(j * rows + i * cont, cont), cont)
                    extra.append(nn(near[i * cont : (i + 1) * cont], v_ref[at, wide(h)]))
                out = out + jnp.concatenate(extra, axis=0)
            total = out[:, HEAD : HEAD + 1]
            outs.append(out[:, :HEAD] * (1.0 / total))
            logs = jnp.where(lanes == h, top + jnp.log2(total), logs)
        o_ref[...] = jnp.concatenate(outs, axis=1).astype(bf16)
        log_ref[...] = logs

    pl.when(j * rows < later)(lambda: run(True))
    pl.when(j * rows >= later)(lambda: run(False))


def attend(q, k, v, later, cont):
    own, cols = q.shape
    rows = min(512, later, own - later)
    block = lambda n: pl.BlockSpec((rows, n), lambda j: (j, 0))
    return pl.pallas_call(
        functools.partial(attend_kernel, later, cont),
        grid=(own // rows,),
        in_specs=[block(cols), whole(k.shape), whole(v.shape)],
        out_specs=[block(PAIR * HEAD), block(128)],
        out_shape=[
            jax.ShapeDtypeStruct((own, PAIR * HEAD), bf16),
            jax.ShapeDtypeStruct((own, 128), f32),
        ],
        compiler_params=params(),
        cost_estimate=cost(8 * own * k.shape[0] * cols // 2, 8 * own * cols),
    )(q, k, v)


def attend_back_kernel(
    later, cont, first, q_ref, k_ref, v_ref, o_ref, log_ref, g_ref, dq_ref, dk_ref, dv_ref, dk, dv
):
    j = pl.program_id(0)
    rows = q_ref.shape[0]

    @pl.when(j == 0)
    def _():
        dk[...] = jnp.zeros_like(dk)
        dv[...] = jnp.zeros_like(dv)

    def run(is_later):
        outs = []
        for h in range(PAIR):
            q = q_ref[:, wide(h)]
            log = log_ref[:, h : h + 1]
            g = g_ref[:, part(first + h)].astype(f32)
            inner = jnp.sum(g * o_ref[:, part(h)].astype(f32), axis=1, keepdims=True)
            g = tail(g, 0.0).astype(bf16)
            k = k_ref[later:, wide(h)]
            probs = jnp.exp2(nt(q, k) - log)
            drift = (probs * (nt(g, v_ref[later:, wide(h)]) - inner)).astype(bf16)
            dv[later:, wide(h)] += tn(probs.astype(bf16), g)
            dk[later:, wide(h)] += tn(drift, q)
            dq = nn(drift, k)
            if is_later:
                extra = []
                for i in range(rows // cont):
                    at = pl.ds(pl.multiple_of(j * rows + i * cont, cont), cont)
                    mine = slice(i * cont, (i + 1) * cont)
                    k = k_ref[at, wide(h)]
                    probs = jnp.where(causal(cont), jnp.exp2(nt(q[mine], k) - log[mine]), 0.0)
                    drift = nt(g[mine], v_ref[at, wide(h)]) - inner[mine]
                    drift = (probs * drift).astype(bf16)
                    dv[at, wide(h)] += tn(probs.astype(bf16), g[mine])
                    dk[at, wide(h)] += tn(drift, q[mine])
                    extra.append(nn(drift, k))
                dq = dq + jnp.concatenate(extra, axis=0)
            outs.append(dq[:, :HEAD] * SCALE)
        dq_ref[...] = jnp.concatenate(outs, axis=1).astype(bf16)

    pl.when(j * rows < later)(lambda: run(True))
    pl.when(j * rows >= later)(lambda: run(False))

    @pl.when(j == pl.num_programs(0) - 1)
    def _():
        outs = [dk[:, h * WIDE : h * WIDE + HEAD] * (1.0 / LOG2E) for h in range(PAIR)]
        dk_ref[...] = jnp.concatenate(outs, axis=1).astype(bf16)
        outs = [dv[:, h * WIDE : h * WIDE + HEAD] for h in range(PAIR)]
        dv_ref[...] = jnp.concatenate(outs, axis=1).astype(bf16)


def attend_back(q, k, v, out, logs, grad, first, later, cont):
    own, cols = q.shape
    total = k.shape[0]
    dense = PAIR * HEAD
    rows = min(512, later, own - later)
    block = lambda n: pl.BlockSpec((rows, n), lambda j: (j, 0))
    return pl.pallas_call(
        functools.partial(attend_back_kernel, later, cont, first),
        grid=(own // rows,),
        in_specs=[block(cols), whole(k.shape), whole(v.shape), block(dense), block(128), block(grad.shape[1])],
        out_specs=[block(dense), whole((total, dense)), whole((total, dense))],
        out_shape=[
            jax.ShapeDtypeStruct((own, dense), bf16),
            jax.ShapeDtypeStruct((total, dense), bf16),
            jax.ShapeDtypeStruct((total, dense), bf16),
        ],
        scratch_shapes=[pltpu.VMEM((total, cols), f32)] * 2,
        compiler_params=params(),
        cost_estimate=cost(1000, 1000),
    )(q, k, v, out, logs, grad)


WEIGHTS = 3


def middle_kernel(counts, info, tok_ref, go_ref, valid_ref, *refs):
    a_refs, refs = refs[:4], refs[4:]
    w_refs, refs = refs[: 4 * len(counts)], refs[4 * len(counts) :]
    ub_ref, y_ref, gm_ref, near_ref, far_ref, sum_ref, keep_ref, send_ref = refs[:8]
    w, acc, att, columns, vectors, sem = refs[8:]
    j = pl.program_id(0)
    cols = a_refs[0].shape[1]
    half = 2 * cols

    @pl.when(j == 0)
    def _():
        acc[...] = jnp.zeros_like(acc)
        sum_ref[...] = jnp.zeros_like(sum_ref)
        for r in range(4):
            spot = 1
            for w_ref in w_refs[r * len(counts) : (r + 1) * len(counts)]:
                count, deep = w_ref.shape[:2]
                for b in range(count):
                    at = pl.ds(pl.multiple_of(info[spot], 16), deep)
                    spot += 1
                    for m in range(WEIGHTS):
                        w[m, at, r * cols : (r + 1) * cols] = w_ref[
                            b, :, m * cols : (m + 1) * cols
                        ]
                    if r == 0:
                        columns[at, 0:4] = w_ref[b, :, 3 * cols : 3 * cols + 4].astype(f32)
        vectors[...] = columns[...].T[:8]

    for r in range(4):
        att[:, r * cols : (r + 1) * cols] = a_refs[r][...]
    attended = att[...]
    mixed = tok_ref[...].astype(f32) + nt(attended, w[0]) + vectors[2:3, :]
    unit, inverse = normalise(mixed)
    gain = vectors[0:1, :]
    normed = (unit * gain + vectors[1:2, :]).astype(bf16)
    upper = nn(normed, w[1]) + ub_ref[...]
    cumulative = 0.5 + 0.5 * lax.erf(upper * (0.5**0.5))
    active = (upper * cumulative).astype(bf16)
    output = mixed + nt(active, w[2]) + vectors[3:4, :]
    y_ref[...] = output.astype(bf16)
    sum_ref[0:1, :] += jnp.sum(output * output * valid_ref[...], axis=0, keepdims=True)

    go = go_ref[...]
    acc[2] += tn(go, active)
    density = jnp.exp(-0.5 * upper * upper) * (1.0 / math.sqrt(2.0 * math.pi))
    grad_upper = nn(go, w[2]) * (cumulative + upper * density)
    sum_ref[5:6, :] += jnp.sum(grad_upper, axis=0, keepdims=True)
    low = grad_upper.astype(bf16)
    acc[1] += tn(normed, low)
    grad_mid = nt(low, w[1])
    sum_ref[2:3, :] += jnp.sum(grad_mid * unit, axis=0, keepdims=True)
    sum_ref[3:4, :] += jnp.sum(grad_mid, axis=0, keepdims=True)
    grad_out = go.astype(f32)
    sum_ref[1:2, :] += jnp.sum(grad_out, axis=0, keepdims=True)
    grad_mixed = grad_out + norm_back(grad_mid, unit, inverse, gain)
    sum_ref[4:5, :] += jnp.sum(grad_mixed, axis=0, keepdims=True)
    gm_ref[...] = grad_mixed
    low = grad_mixed.astype(bf16)
    acc[0] += tn(low, attended)
    grad_attended = nn(low, w[0]).astype(bf16)
    near_ref[...] = grad_attended[:, :half]
    far_ref[...] = grad_attended[:, half:]

    @pl.when(j == pl.num_programs(0) - 1)
    def _():
        copies = []
        for m in range(WEIGHTS):
            w[m] = acc[m].astype(bf16)
            for i, out_ref in enumerate((keep_ref, send_ref)):
                source = w.at[m, :, pl.ds(i * half, half)]
                target = out_ref.at[:, pl.ds(m * half, half)]
                copies.append(pltpu.make_async_copy(source, target, sem.at[2 * m + i]))
                copies[-1].start()
        for copy in copies:
            copy.wait()


def middle(info, tokens, grad, valid, mine, theirs, weights, up_bias, rows, half):
    count, width = tokens.shape
    cols = mine[0].shape[1]
    per = half // rows
    block = lambda n: pl.BlockSpec((rows, n), lambda j, info: (j, 0))
    own = pl.BlockSpec(
        (rows, cols), lambda j, info: ((2 * (j // per) + info[0]) * per + j % per, 0)
    )
    flat = [w for group in weights for w in group]
    hbm = pl.BlockSpec(memory_space=pl.ANY)
    shape = jax.ShapeDtypeStruct
    return pl.pallas_call(
        functools.partial(middle_kernel, [w.shape[0] for w in weights[0]]),
        grid_spec=pltpu.PrefetchScalarGridSpec(
            num_scalar_prefetch=1,
            grid=(count // rows,),
            in_specs=[block(width), block(width), block(1), own, own, block(cols), block(cols)]
            + [once(w.shape) for w in flat]
            + [whole(up_bias.shape)],
            out_specs=[block(width), block(width), block(2 * cols), block(2 * cols)]
            + [whole((8, width)), hbm, hbm],
            scratch_shapes=[
                pltpu.VMEM((WEIGHTS, width, 4 * cols), bf16),
                pltpu.VMEM((WEIGHTS, width, 4 * cols), f32),
                pltpu.VMEM((rows, 4 * cols), bf16),
                pltpu.VMEM((width, 128), f32),
                pltpu.VMEM((8, width), f32),
                pltpu.SemaphoreType.DMA((2 * WEIGHTS,)),
            ],
        ),
        out_shape=[
            shape((count, width), bf16),
            shape((count, width), f32),
            shape((count, 2 * cols), bf16),
            shape((count, 2 * cols), bf16),
            shape((8, width), f32),
            shape((width, 2 * WEIGHTS * cols), bf16),
            shape((width, 2 * WEIGHTS * cols), bf16),
        ],
        compiler_params=params(),
        cost_estimate=cost(148 * count * width * cols, 30 * count * width),
    )(info, tokens, grad, valid, *mine, *theirs, *flat, up_bias)


BEYOND, BEYOND_TOO, THEIRS, MINE = 0, 1, 2, 3


def project_back_kernel(sums, spans, more, adding, placing, counts, info, *refs):
    x_ref, dq_ref, dk_ref, dv_ref = refs[:4]
    refs = refs[4:]
    w_refs, refs = refs[: len(counts)], refs[len(counts) :]
    prev_refs, refs = refs[:more], refs[more:]
    other, refs = refs[:adding], refs[adding:]
    shares, refs = refs[:placing], refs[placing:]
    outs, refs = refs[: len(spans)], refs[len(spans) :]
    d = refs[-3] if placing else refs[-1]
    j = pl.program_id(0)
    cols = dq_ref.shape[1]
    if spans:
        w = refs[-2]

        @pl.when(j == 0)
        def _():
            spot = 1
            for w_ref in w_refs:
                count, deep = w_ref.shape[:2]
                for b in range(count):
                    at = pl.ds(pl.multiple_of(info[spot], 16), deep)
                    w[at, : 3 * cols] = w_ref[b, :, : 3 * cols]
                    spot += 1
            w[:, 3 * cols :] = jnp.zeros_like(w[:, 3 * cols :])

    @pl.when(j == 0)
    def _():
        d[:, 3 * cols :] = jnp.zeros_like(d[:, 3 * cols :])

    asked = info[1 + sum(counts)]

    @pl.when(j < asked)
    def _():
        d[:, :cols] = jnp.zeros_like(dq_ref)

    @pl.when(j >= asked)
    def _():
        d[:, :cols] = dq_ref[...]

    d[:, cols : 2 * cols] = dk_ref[...]
    d[:, 2 * cols : 3 * cols] = dv_ref[...]
    all_d = d[...]
    if sums:
        dw_refs, refs = refs[:sums], refs[sums:]
        if placing:
            targets, (stage, sem) = refs[1:3], refs[-2:]
            refs = (refs[0], *refs[3:-2])
            half = stage.shape[1]
            c, y = info[0], info[2 + sum(counts)]
            loads, stores = [], []
            for i, share in enumerate(shares):
                spot = pl.ds(pl.multiple_of((c ^ (i % 2)) * half, 16), half)
                for kind, target in enumerate(targets):
                    n = 2 * i + kind
                    source, place = share.at[pl.ds(kind * half, half)], stage.at[n]
                    loads.append(pltpu.make_async_copy(source, place, sem.at[0, n]))
                    place = target.at[y ^ (i // 2), spot]
                    stores.append(pltpu.make_async_copy(stage.at[n], place, sem.at[1, n]))

            @pl.when(j == 0)
            def _():
                for copy in loads:
                    copy.start()

            @pl.when(j == 2)
            def _():
                for load, store in zip(loads, stores):
                    load.wait()
                    store.start()

            @pl.when(j == pl.num_programs(0) - 1)
            def _():
                for copy in stores:
                    copy.wait()

        sum_ref, acc = refs[:2]

        @pl.when(j == 0)
        def _():
            acc[...] = jnp.zeros_like(acc)
            sum_ref[...] = jnp.zeros_like(sum_ref)

        acc[...] += tn(x_ref[...], all_d)
        sum_ref[0:1, :] += jnp.sum(all_d.astype(f32), axis=0, keepdims=True)

        @pl.when(j == pl.num_programs(0) - 1)
        def _():
            at = 0
            for piece in other:
                acc[:, at : at + piece.shape[1]] += piece[...].astype(f32)
                at += piece.shape[1]
            at = 0
            for dw_ref in dw_refs:
                dw_ref[...] = acc[:, at : at + dw_ref.shape[1]].astype(bf16)
                at += dw_ref.shape[1]

    if spans:
        grad = nt(all_d, w[...])
        for i, (low, high) in enumerate(spans):

            @pl.when((j >= low) & (j < high))
            def _():
                if more:
                    outs[i][...] = (grad + prev_refs[i][...].astype(f32)).astype(bf16)
                else:
                    outs[i][...] = grad.astype(bf16)


def tiled(count):
    return -(-count // 256) * 256


def project_back(
    sums, wanted, c, y, starts, x, dq, dk, dv, weights, previous, rows, half, own, other, shares
):
    total, width = x.shape
    cols = dq.shape[1]
    sizes = ((total - own) // 2 // rows,) * 2 + (own // 2 // rows,) * 2
    n_beyond = 2 * sizes[0] if BEYOND in wanted else 0
    n_half = sizes[2]
    per = half // rows
    steps = sum(sizes[i] for i in wanted)
    info = jnp.stack([jnp.asarray(v, jnp.int32) for v in (c, *starts, n_beyond, y)])

    def row(j, info):
        i = j - n_beyond
        share = (i >= n_half).astype(jnp.int32)
        i = i - share * n_half
        side = jnp.where(share == 1, info[0], 1 - info[0])
        inner = (2 * (i // per) + side) * per + i % per
        return jnp.where(j < n_beyond, own // rows + j, inner)

    def dq_row(j, info):
        return jnp.minimum(row(jnp.maximum(j, n_beyond), info), own // rows - 1)

    x_spec = pl.BlockSpec((rows, width), lambda j, info: (row(j, info), 0))
    d_spec = pl.BlockSpec((rows, cols), lambda j, info: (row(j, info), 0))
    q_spec = pl.BlockSpec((rows, cols), lambda j, info: (dq_row(j, info), 0))
    parts, spans, low = [], [], 0
    if previous is not None:
        for i in wanted:
            n = sizes[i]
            spans.append((low, low + n))
            parts.append(
                pl.BlockSpec(
                    (rows, width),
                    functools.partial(lambda a, b, j, info: (jnp.clip(j - a, 0, b - 1), 0), low, n),
                )
            )
            low += n
    shape = jax.ShapeDtypeStruct
    out_specs = list(parts)
    out_shape = [shape((sizes[i] * rows, width), bf16) for i in wanted[: len(parts)]]
    scratch = []
    lanes = tiled(3 * cols)
    if sums:
        out_specs += [whole((width, n)) for n in sums] + [whole((8, lanes))]
        out_shape += [shape((width, n), bf16) for n in sums] + [shape((8, lanes), f32)]
        scratch.append(pltpu.VMEM((width, lanes), f32))
    hbm = pl.BlockSpec(memory_space=pl.ANY)
    if shares:
        out_specs += [hbm, hbm]
        out_shape += [shape((2, own // 2, width), bf16)] * 2
    if parts:
        scratch.append(pltpu.VMEM((width, lanes), bf16))
    scratch.append(pltpu.VMEM((rows, lanes), bf16))
    if shares:
        scratch.append(pltpu.VMEM((2 * len(shares), half, width), bf16))
        scratch.append(pltpu.SemaphoreType.DMA((2, 2 * len(shares))))
    return pl.pallas_call(
        functools.partial(
            project_back_kernel,
            len(sums),
            spans,
            len(previous or []),
            len(other),
            len(shares),
            [w.shape[0] for w in weights],
        ),
        grid_spec=pltpu.PrefetchScalarGridSpec(
            num_scalar_prefetch=1,
            grid=(steps,),
            in_specs=[x_spec, q_spec, d_spec, d_spec]
            + [once(w.shape) for w in weights]
            + (parts if previous else [])
            + [once(o.shape) for o in other]
            + [hbm] * len(shares),
            out_specs=out_specs,
            scratch_shapes=scratch,
        ),
        out_shape=out_shape,
        compiler_params=params(),
        cost_estimate=cost(1000, 1000),
    )(info, x, dq, dk, dv, *weights, *(previous or []), *other, *shares)


def finish_kernel(n, gain_ref, tok_ref, mix_ref, *refs):
    shares, (low_ref, sum_ref) = refs[:n], refs[n:]

    @pl.when(pl.program_id(0) == 0)
    def _():
        sum_ref[...] = jnp.zeros_like(sum_ref)

    grad = shares[0][...].astype(f32)
    for share in shares[1:]:
        grad = grad + share[...].astype(f32)
    unit, inverse = normalise(tok_ref[...].astype(f32))
    back = norm_back(grad, unit, inverse, gain_ref[0:1, :])
    low_ref[...] = (mix_ref[...] + back).astype(bf16)
    sum_ref[0:1, :] += jnp.sum(grad * unit, axis=0, keepdims=True)
    sum_ref[1:2, :] += jnp.sum(grad, axis=0, keepdims=True)


def finish(kind, gain, tokens, mixed, shares, back, half):
    width = tokens.shape[1]
    rows = min(128, half)
    n = half // rows
    block = pl.BlockSpec((rows, width), lambda j: (kind * n + j, 0))
    plain = pl.BlockSpec((rows, width), lambda j: (j, 0))
    return pl.pallas_call(
        functools.partial(finish_kernel, len(shares) + len(back)),
        grid=(n,),
        in_specs=[whole(gain.shape), block, block] + [block] * len(shares) + [plain] * len(back),
        out_specs=[plain, whole((8, width))],
        out_shape=[
            jax.ShapeDtypeStruct((half, width), bf16),
            jax.ShapeDtypeStruct((8, width), f32),
        ],
        compiler_params=params(),
        cost_estimate=cost(1000, 1000),
    )(gain, tokens, mixed, *shares, *back)


def assemble_kernel(count, info, *refs):
    i = pl.program_id(0)
    for m in range(count):

        @pl.when(i == m)
        def _():
            refs[-1][...] = refs[m][...].astype(refs[-1].dtype)[None]


def assemble(info, pieces, kind, half, dtype, first=0, into=()):
    width = pieces[0].shape[1]
    count = len(pieces)
    return pl.pallas_call(
        functools.partial(assemble_kernel, count),
        grid_spec=pltpu.PrefetchScalarGridSpec(
            num_scalar_prefetch=1,
            grid=(count,),
            in_specs=[pl.BlockSpec((half, width), lambda i, info: (kind, 0))] * count
            + [pl.BlockSpec(memory_space=pl.ANY)] * len(into),
            out_specs=pl.BlockSpec(
                (1, half, width),
                lambda i, info: (info[0] ^ ((first + i) // 2), info[1] ^ ((first + i) % 2), 0),
            ),
        ),
        out_shape=jax.ShapeDtypeStruct((2, 2 * half, width), dtype),
        input_output_aliases={count + 1: 0} if into else {},
        compiler_params=params(),
        cost_estimate=cost(1000, 1000),
    )(info, *pieces, *into)


def swap(value, axis, bit):
    count = lax.axis_size(axis)
    return lax.ppermute(value, axis, [(i, i ^ bit) for i in range(count)])


def pick(array, index, axis=0):
    return lax.dynamic_index_in_dim(array, index, axis, keepdims=False)


def in_order(index, mine, theirs, axis=0):
    first = index == 0
    return jnp.stack(
        [jnp.where(first, mine, theirs), jnp.where(first, theirs, mine)], axis=axis
    )


def direct():
    return lax.axis_size(C) == 2 and lax.axis_size(S) == 4


def phase(*values):
    return lax.optimization_barrier(values)


def over_z(piece):
    return [swap(piece, S, i) for i in (1, 2, 3)]


def z_parts(rows, axis):
    z = lax.axis_index(S)
    low = rows.astype(bf16)
    return [pick(low, z ^ i, axis) for i in (1, 2, 3)], pick(rows, z, axis)


def z_sum(mine, parts):
    for piece in parts:
        mine = mine + piece.astype(f32)
    return mine


def z_moves(parts):
    return [swap(piece, S, i + 1) for i, piece in enumerate(parts)]


def x_parts(rows, axis):
    x = lax.axis_index(C)
    shape = rows.shape
    split = rows.reshape(*shape[:axis], 4, 2, shape[axis] // 8, *shape[axis + 1 :])
    return pick(split, 1 - x, axis + 1).astype(bf16), pick(split, x, axis + 1)


def sum_over(values, axis):
    count, bit = lax.axis_size(axis), 1
    while bit < count:
        values = values + swap(values, axis, bit)
        bit *= 2
    return values


def body(
    prompt_tokens,
    later_tokens,
    prompt_upstream,
    later_upstream,
    prompt_lengths,
    later_lengths,
    query_weight,
    key_weight,
    value_weight,
    out_weight,
    up_weight,
    down_weight,
    pre_gain,
    pre_shift,
    mid_gain,
    mid_shift,
    query_bias,
    value_bias,
    out_bias,
    up_bias,
    down_bias,
):
    groups, prompt_rows, width = prompt_tokens.shape
    count, cont = later_tokens.shape[1:3]
    later = count * cont
    own = later + prompt_rows
    contexts = lax.axis_size(C)
    total = later + prompt_rows * contexts
    cols = query_weight.shape[1]
    half = later // 2
    big = min(512, later)
    x = lax.axis_index(C)
    t = lax.axis_index(T)
    y, c = t // 2, t % 2
    turn = (t, t ^ 2, t ^ 1, t ^ 3)

    def share(array, side):
        rows = array.reshape(2, 2, half, array.shape[-1])
        return pick(rows, side, 1).reshape(2 * half, array.shape[-1])

    prompt = pick(prompt_tokens, y)
    qkv_piece = jnp.concatenate(
        [query_weight, key_weight, value_weight, pre_gain[:, None], pre_shift[:, None]], axis=1
    )
    oud_piece = jnp.concatenate(
        [out_weight.T, up_weight, down_weight.T]
        + [v[:, None] for v in (mid_gain, mid_shift, out_bias, down_bias)],
        axis=1,
    )
    length = pick(prompt_lengths, y)
    lengths = pick(later_lengths, y)
    follow = pick(later_tokens, y).reshape(later, width)
    row_tokens = share(jnp.concatenate([follow, prompt], axis=0), c)
    later_valid = jnp.arange(cont, dtype=jnp.int32)[None, :] < lengths[:, None]
    prompt_valid = x * prompt_rows + jnp.arange(prompt_rows, dtype=jnp.int32) < length
    valid = jnp.concatenate([later_valid.reshape(later), prompt_valid]).astype(f32)
    valid = share(valid[:, None], c)
    upstream = jnp.concatenate(
        [pick(later_upstream, y).reshape(later, width), pick(prompt_upstream, y)], axis=0
    )
    grad_low = (share(upstream, c).astype(f32) * valid).astype(bf16)

    biases = jnp.concatenate([query_bias, value_bias, up_bias])[None]
    if direct():
        z = lax.axis_index(S)
        deep = query_weight.shape[0]
        starts = [((z ^ i) * 2 + (x ^ k)) * deep for k in (0, 1) for i in range(4)]
        places = [(1 - x) * prompt_rows + side * half for side in (c, 1 - c)]
        tokens_piece = pick(prompt_tokens.reshape(groups * 2, half, width), 2 * y + c)
        tokens_piece, qkv_piece = phase(tokens_piece, qkv_piece)
        tokens_piece = swap(tokens_piece, C, 1)
        parts = over_z(qkv_piece)
        rows = jnp.pad(biases, ((0, 15), (0, qkv_piece.shape[1] - biases.shape[1])))
        far_piece = swap(jnp.concatenate([qkv_piece, rows]), T, 2)
        far_piece, tokens_piece, oud_piece, row_tokens, grad_low, valid, *parts = phase(
            far_piece, tokens_piece, oud_piece, row_tokens, grad_low, valid, *parts
        )
        far_biases = far_piece[deep : deep + 1, : biases.shape[1]]
        far_piece = far_piece[:deep]
        near = jnp.stack([qkv_piece, *parts])
        qkv_own = [near, swap(near, C, 1)]
        beyond = [tokens_piece, swap(tokens_piece, T, 1)]
        parts = [far_piece, *over_z(far_piece)]
        parts = phase(*qkv_own, *beyond, *parts, oud_piece)
        qkv_own, beyond, oud_piece = list(parts[:2]), list(parts[2:4]), parts[8]
        near = jnp.stack(parts[4:8])
        qkv_far = [near, swap(near, C, 1)]
        oud_parts = over_z(oud_piece)
    else:
        starts = [0]
        rolled = jnp.roll(lax.all_gather(prompt, C), -x, axis=0)[1:]
        beyond = [rolled.reshape(-1, width)]
        places = [((x + i) % contexts) * prompt_rows for i in range(1, contexts)]
        qkv_own = [lax.all_gather(qkv_piece, SC, axis=0, tiled=True)[None]]
        qkv_far = [swap(w, T, 2) for w in qkv_own]
        far_biases = swap(biases, T, 2)
    biases = jnp.concatenate([biases, far_biases]).astype(f32)

    def ints(*values):
        return jnp.stack([jnp.asarray(v, jnp.int32) for v in values])

    blocks = [-1] * (later // big)
    blocks += [x * prompt_rows + i * big for i in range(prompt_rows // big)]
    blocks += [p + i * big for p in places for i in range(max(half if direct() else prompt_rows, big) // big)]
    info = ints(y, length, *starts, *blocks)

    q0, k0, v0, normed_in, pre_vectors = project(
        True,
        info,
        [later_tokens.reshape(groups, later, width), prompt_tokens] + beyond,
        qkv_own,
        biases[0:1, :cols],
        biases[0:1, cols : 2 * cols],
        big,
        own,
        total,
    )
    if direct():
        q0, k0, v0, normed_in, *parts = phase(q0, k0, v0, normed_in, *qkv_far, *oud_parts)
        qkv_far = parts[:2]
        near = jnp.stack([oud_piece, *parts[2:]])
        oud_own = [near, swap(near, C, 1)]
        near = swap(near, T, 2)
    a0, log0 = attend(q0, k0, v0, later, cont)
    if direct():
        a0, near, *oud_own = phase(a0, near, *oud_own)
        oud_far = [near, swap(near, C, 1)]
    else:
        oud_own = [lax.all_gather(oud_piece, SC, axis=0, tiled=True)[None]]
        oud_far = [swap(w, T, 2) for w in oud_own]
    oud = [oud_own, oud_far] + [[swap(w, T, 1) for w in ws] for ws in (oud_own, oud_far)]
    r0 = swap(share(a0, 1 - c), T, 1)
    up_bias = biases[:, 2 * cols :]
    up_bias = jnp.concatenate([up_bias, swap(up_bias, T, 1)]).reshape(1, -1)
    q1, k1, v1 = project(
        False,
        info,
        [normed_in],
        qkv_far,
        biases[1:2, :cols],
        biases[1:2, cols : 2 * cols],
        big,
        own,
        total,
    )
    if direct():
        q1, k1, v1, oud[2][0], oud[2][1], oud[3][0], r0, up_bias = phase(
            q1, k1, v1, oud[2][0], oud[2][1], oud[3][0], r0, up_bias
        )
    a1, log1 = attend(q1, k1, v1, later, cont)
    if direct():
        a1, oud_far[1] = phase(a1, oud_far[1])
        oud[3][1] = swap(oud_far[1], T, 1)
    r1 = swap(share(a1, 1 - c), T, 1)

    output, grad_mixed, grad_near, grad_away, sums, oud_keep, oud_send = middle(
        ints(c, *starts),
        row_tokens,
        grad_low,
        valid,
        [a0, a1],
        [r0, r1],
        oud,
        up_bias,
        min(256, half),
        half,
    )

    where = ints(y, c)
    back_rows = min(512, half)
    everything = (BEYOND, BEYOND_TOO, THEIRS, MINE)
    lanes = tiled(3 * cols)
    far_widths = (3 * lanes // 4, lanes // 4)
    received = swap(grad_away, T, 1)
    grad_heads = in_order(
        c, grad_near.reshape(2, half, -1), received.reshape(2, half, -1), 1
    ).reshape(own, -1)
    if direct():
        grad_heads, oud_send, output = phase(grad_heads, oud_send, output)
    oud_send = swap(oud_send, T, 1)
    outputs = [output, swap(output, T, 1), swap(output, T, 2), None]

    def back_from(q, k, v, out, logs, weights, first):
        def run(grads):
            return attend_back(q, k, v, out, logs, grads, first, later, cont)

        def inputs(grads, wanted, widths, previous, other=(), shares=()):
            return project_back(
                widths,
                wanted,
                c,
                y,
                starts,
                normed_in,
                *grads,
                weights,
                previous,
                back_rows,
                half,
                own,
                other,
                shares,
            )

        return run, inputs

    far_attend, far_back = back_from(q1, k1, v1, a1, log1, qkv_far, PAIR)
    near_attend, near_back = back_from(q0, k0, v0, a0, log0, qkv_own, 0)

    grads = far_attend(grad_heads)
    if direct():
        *grads, oud_keep, oud_send = phase(*grads, oud_keep, oud_send)
    oud_parts = [slice(0, min(1024, oud_send.shape[1])), slice(min(1024, oud_send.shape[1]), None)]
    oud_parts = [oud_keep[:, p].astype(f32) + oud_send[:, p].astype(f32) for p in oud_parts]
    if direct():
        away, kept = zip(*[x_parts(p, 0) for p in oud_parts])
        kept = [k.astype(bf16) for k in kept]
        *grads, kept[0], kept[1], away0, away1 = phase(*grads, *kept, *away)
        away0 = swap(away0, C, 1)
    *shares, far, far_rest, sums1 = far_back(grads, everything, far_widths, [])
    if direct():
        far, far_rest, grad_heads, away0, away1, outputs[1], outputs[2] = phase(
            far, far_rest, grad_heads, away0, away1, outputs[1], outputs[2]
        )
        parts, first_sum = z_parts(kept[0].astype(f32) + away0.astype(f32), 0)
        grad_heads, far, away1, first_sum, *parts = phase(grad_heads, far, away1, first_sum, *parts)
        away1 = swap(away1, C, 1)
        first_parts = z_moves(parts)
    far = swap(far, T, 2)
    grads = near_attend(grad_heads)
    if direct():
        *grads, far, far_rest, away1, first_sum, outputs[2], p1, p2, p3 = phase(
            *grads, far, far_rest, away1, first_sum, outputs[2], *first_parts
        )
        first_done = [p1, p2, p3]
        parts, last_sum = z_parts(kept[1].astype(f32) + away1.astype(f32), 0)
        g0, far_rest, first_sum, last_sum, *parts = phase(
            grads[0], far_rest, first_sum, last_sum, *parts
        )
        grads[0] = g0
        last_parts = z_moves(parts)
    far_rest = swap(far_rest, T, 2)
    outputs[3] = swap(outputs[2], T, 1)
    if direct():
        b0, b1, their_share, my_share = near_back(grads, everything, (), shares)
        b0, b1, their_share, my_share, first_sum, last_sum, far, far_rest, *parts = phase(
            b0,
            b1,
            their_share,
            my_share,
            first_sum,
            last_sum,
            far,
            far_rest,
            grads[0],
            outputs[3],
            *first_done,
            *last_parts,
        )
        grads[0], outputs[3] = parts[:2]
        their_share, b1 = swap(their_share, T, 1), swap(b1, T, 1)
        first_sum, last_sum = z_sum(first_sum, parts[2:5]), z_sum(last_sum, parts[5:])
        oud_grad = jnp.concatenate([first_sum, last_sum], axis=1).astype(bf16)
        oud_far = oud_grad.reshape(-1, WEIGHTS, 2, cols)[:, :, 1]
        my_share, their_share, b0, b1, oud_grad, oud_far = phase(
            my_share, their_share, b0, b1, oud_grad, oud_far
        )
        oud_far = swap(oud_far, T, 2)
        back = swap((b0.astype(f32) + b1.astype(f32)).astype(bf16), C, 1)
        shares = [my_share, their_share]
        low, sums_later = finish(0, pre_vectors, row_tokens, grad_mixed, shares, [], half)
        low, sums_later, shares[0], shares[1], oud_far, far, far_rest, g0, *outputs = phase(
            low, sums_later, *shares, oud_far, far, far_rest, grads[0], *outputs
        )
        grads[0] = g0
        pieces = [low, swap(low, T, 1), swap(low, T, 2), None]
        widths = (5 * lanes // 8, 3 * lanes // 8)
        *near, sums0, later_output, prompt_output = near_back(
            grads, everything, widths, None, (far, far_rest), outputs
        )
        x_away, x_kept = x_parts(near[0], 0)
        z_split = near[1].reshape(4, 2 * deep, widths[1])
        parts, z_kept = [pick(z_split, z ^ i) for i in (1, 2, 3)], pick(z_split, z)
        x_away, x_kept, z_kept, sums0, pieces[1], *parts = phase(
            x_away, x_kept, z_kept, sums0, pieces[1], *parts
        )
        x_away = swap(x_away, C, 1)
        z_away = z_moves(parts)
        back, pieces[2] = phase(back, pieces[2])
        pieces[3] = swap(pieces[2], T, 1)
        low, sums_prompt = finish(1, pre_vectors, row_tokens, grad_mixed, shares, [back], half)
    else:
        oud_grad = jnp.concatenate([p.astype(bf16) for p in oud_parts], axis=1)
        b0, b1, their_share, my_share, near, sums0 = near_back(
            grads, everything, (lanes,), shares, (far, far_rest)
        )
        shares = [my_share, swap(their_share, T, 1)]
        back = jnp.concatenate([b0, b1])
        back = back.astype(f32) + swap(back, T, 1).astype(f32)
        back = back.reshape(contexts - 1, prompt_rows, width)
        back = jnp.concatenate([jnp.zeros_like(back[:1]), back], axis=0)
        back = jnp.roll(back, x, axis=0).astype(bf16)
        back = lax.psum_scatter(back, C, scatter_dimension=0, tiled=True)
        back = pick(back.reshape(2, half, width), c)
        low, sums_later = finish(0, pre_vectors, row_tokens, grad_mixed, shares, [], half)
        pieces = [low, None, swap(low, T, 2), None]
        low, sums_prompt = finish(1, pre_vectors, row_tokens, grad_mixed, shares, [back], half)
        later_output = assemble(where, outputs, 0, half, bf16)
        prompt_output = assemble(where, outputs, 1, half, bf16)
        qkv_grad, oud_grad = [
            lax.psum_scatter(g, SC, scatter_dimension=0, tiled=True) for g in (near, oud_grad)
        ]
        qkv_grad = qkv_grad.astype(f32)

    def placed(*pieces):
        block = lax.broadcasted_iota(jnp.int32, (lax.axis_size(T), cols), 0)
        return sum(jnp.where(block == i, v[None], 0.0) for i, v in zip(turn, pieces)).reshape(-1)

    row = lax.broadcasted_iota(jnp.int32, (8, width), 0)
    lane = lax.broadcasted_iota(jnp.int32, (8, width), 1)
    group = lax.axis_index(S) * groups + y
    every = lax.axis_size(S) * groups
    scalars = jnp.where(lane == group, jnp.sum(sums[0]), 0.0)
    scalars = jnp.where(lane == every + group, jnp.sum(valid), scalars)
    up_sums = placed(*sums[5].reshape(4, cols))
    sums = jnp.where(row == 6, scalars, jnp.where(row == 7, up_sums[None], sums))
    q_sums = placed(sums0[0, :cols], sums1[0, :cols])
    v_sums = placed(sums0[0, 2 * cols : 3 * cols], sums1[0, 2 * cols : 3 * cols])
    more = jnp.where(row == 2, q_sums[None], jnp.where(row == 3, v_sums[None], sums_later))
    if direct():
        low, sums_prompt, sums, more, oud_grad, oud_far, x_away, x_kept, z_kept, *rest = phase(
            low,
            sums_prompt,
            sums,
            more,
            oud_grad,
            oud_far,
            x_away,
            x_kept,
            z_kept,
            *pieces,
            *z_away,
        )
        pieces, z_away = rest[:4], rest[4:]
    sums = jnp.concatenate([sums, more + sums_prompt])
    sums = sums + swap(sums, T, 2)
    if direct():
        low, sums = phase(low, sums)
    last = [low, swap(low, T, 1), swap(low, T, 2), None]
    if direct():
        z_first = z_sum(z_kept.astype(f32), z_away).reshape(2, deep, widths[1])
        z_away, z_first = pick(z_first, 1 - x).astype(bf16), pick(z_first, x)
        parts, x_first = z_parts(x_kept.astype(f32) + x_away.astype(f32), 0)
        z_away, z_first, x_first, pieces[0], *parts = phase(
            z_away, z_first, x_first, pieces[0], *parts
        )
        parts = z_moves(parts)
        arrived, z_away = swap(sums, T, 1), swap(z_away, C, 1)
        later_grad = assemble(where, pieces, 0, half, f32)
        later_grad, sums, arrived, z_away, last[1], x_first, *parts = phase(
            later_grad, sums, arrived, z_away, last[1], x_first, *parts
        )
        sums = sums + arrived
        sums, last[1], x_first, *parts = phase(sums, last[1], x_first, *parts)
        arrived = swap(sums, C, 1)
        prompt_grad = assemble(where, last[:2], 0, half, f32)
        qkv_grad = jnp.concatenate(
            [z_sum(x_first, parts), z_first + z_away.astype(f32)], axis=1
        )
        sums = sum_over(sums + arrived, S)
        prompt_grad, sums, last[2], qkv_grad = phase(prompt_grad, sums, last[2], qkv_grad)
    else:
        pieces[1] = swap(pieces[0], T, 1)
        pieces[3] = swap(pieces[2], T, 1)
        later_grad = assemble(where, pieces, 0, half, f32)
        prompt_grad = assemble(where, last[:2], 0, half, f32)
        sums = sum_over(sum_over(sums + swap(sums, T, 1), C), S)
    oud_grad = oud_grad.reshape(-1, WEIGHTS, 2, cols)
    if not direct():
        oud_far = swap(oud_grad[:, :, 1], T, 2)
    oud_grad = oud_grad[:, :, 0].astype(f32) + oud_far.astype(f32)
    last[3] = swap(last[2], T, 1)
    squares = lax.dynamic_slice(sums[6], (lax.axis_index(S) * groups,), (groups,))
    counted = lax.dynamic_slice(sums[6], (every + lax.axis_index(S) * groups,), (groups,))
    magnitude = jnp.sqrt(squares / (counted * width))
    prompt_grad = assemble(where, last[2:], 0, half, f32, 2, [prompt_grad])
    n = width // (lax.axis_size(S) * contexts)
    place = lax.axis_index(S) * contexts + x

    def own_vector(row):
        return lax.dynamic_slice(row, (place * n,), (n,))

    def own_heads(row):
        return lax.dynamic_slice(row, (t * cols,), (cols,))

    shaped = (groups, count, cont, width)
    return (
        prompt_output,
        later_output.reshape(shaped),
        prompt_grad,
        later_grad.reshape(shaped),
        qkv_grad[:, :cols],
        qkv_grad[:, cols : 2 * cols],
        qkv_grad[:, 2 * cols : 3 * cols],
        oud_grad[:, 0].T,
        oud_grad[:, 1],
        oud_grad[:, 2].T,
        own_vector(sums[8]),
        own_vector(sums[9]),
        own_vector(sums[2]),
        own_vector(sums[3]),
        own_heads(sums[10]),
        own_heads(sums[11]),
        own_vector(sums[4]),
        own_heads(sums[7]),
        own_vector(sums[1]),
        magnitude,
    )


def solution(mesh):
    rows, later, vector = P(S, C, None), P(S, C, None, None), P(SC)
    weight, turned, column = P(SC, T), P(T, SC), P(T)
    return jax.shard_map(
        body,
        mesh=mesh,
        in_specs=(rows, later, rows, later, P(S), P(S, C))
        + (weight, weight, weight, turned, weight, turned)
        + (vector,) * 4
        + (column, column, vector, column, vector),
        out_specs=(rows, later, rows, later)
        + (weight, weight, weight, turned, weight, turned)
        + (vector,) * 4
        + (column, column, vector, column, vector, P(S)),
        check_vma=False,
    )
```

```python
import functools
import math

import jax
import jax.numpy as jnp
from jax import lax
from jax.experimental import pallas as pl
from jax.experimental.pallas import tpu as pltpu
from jax.sharding import PartitionSpec as P

S, C, T = "shard", "context", "tensor"
SC = (S, C)
ALL = (S, C, T)
HEAD = 160
WIDE = 256
PAIR = 2
EPSILON = 1e-05
MASKED = -1e30
SCALE = HEAD**-0.5
LOG2E = math.log2(math.e)
VMEM = 58 * 1024 * 1024
bf16 = jnp.bfloat16
f32 = jnp.float32


def nt(a, b):
    return lax.dot_general(a, b, (((1,), (1,)), ((), ())), preferred_element_type=f32)


def nn(a, b):
    return lax.dot_general(a, b, (((1,), (0,)), ((), ())), preferred_element_type=f32)


def tn(a, b):
    return lax.dot_general(a, b, (((0,), (0,)), ((), ())), preferred_element_type=f32)


def normalise(values):
    centre = values - jnp.mean(values, axis=-1, keepdims=True)
    spread = jnp.mean(centre * centre, axis=-1, keepdims=True)
    inverse = lax.rsqrt(spread + EPSILON)
    return centre * inverse, inverse


def norm_back(grad, unit, inverse, gain):
    e = grad * gain
    inner = e - jnp.mean(e, axis=-1, keepdims=True)
    return (inner - unit * jnp.mean(e * unit, axis=-1, keepdims=True)) * inverse


def part(h):
    return slice(h * HEAD, (h + 1) * HEAD)


def wide(h):
    return slice(h * WIDE, (h + 1) * WIDE)


def tail(values, first):
    lane = lax.broadcasted_iota(jnp.int32, (values.shape[0], WIDE - HEAD), 1)
    return jnp.concatenate([values, jnp.where(lane == 0, first, 0.0)], axis=1)


def params(count=1):
    return pltpu.CompilerParams(
        vmem_limit_bytes=VMEM, dimension_semantics=("arbitrary",) * count
    )


def whole(shape):
    return pl.BlockSpec(shape, lambda j, *_: (0,) * len(shape))


def once(shape):
    return pl.BlockSpec(
        shape, lambda j, *_: (0,) * len(shape), pipeline_mode=pl.Buffered(1)
    )


def cost(flops, moved, exps=0):
    return pl.CostEstimate(flops=int(flops), bytes_accessed=int(moved), transcendentals=0)


def project_kernel(fresh, own, spans, weights, info, *refs):
    x_refs, refs = refs[: len(spans)], refs[len(spans) :]
    w_refs, refs = refs[: len(weights)], refs[len(weights) :]
    qb_ref, vb_ref, q_ref, k_ref, v_ref = refs[:5]
    w_pad, columns = refs[-2:]
    vectors = refs[6] if fresh else None
    dense = 3 * PAIR * HEAD
    j = pl.program_id(0)
    rows = k_ref.shape[0]

    @pl.when(j == 0)
    def _():
        w_pad[...] = jnp.zeros_like(w_pad)
        spot = 2
        for w_ref in w_refs:
            count, deep = w_ref.shape[:2]
            for b in range(count):
                at = pl.ds(pl.multiple_of(info[spot], 16), deep)
                spot += 1
                for i in range(3 * PAIR):
                    w_pad[at, i * WIDE : i * WIDE + HEAD] = w_ref[b, :, part(i)]
                if fresh:
                    columns[at, 0:2] = w_ref[b, :, dense : dense + 2].astype(f32)
        if fresh:
            vectors[...] = columns[...].T[:8]

    if fresh:
        n_ref = refs[5]
        for x_ref, (low, high) in zip(x_refs, spans):

            @pl.when((j >= low) & (j < high))
            def _():
                unit, _ = normalise(x_ref[...].reshape(rows, -1).astype(f32))
                n_ref[...] = (unit * vectors[0:1, :] + vectors[1:2, :]).astype(bf16)

        normed = n_ref[...]
    else:
        normed = x_refs[0][...]

    @pl.when(j * rows < own)
    def _():
        for h in range(PAIR):
            row = tail(qb_ref[:, part(h)] * (SCALE * LOG2E), 1.0)
            product = nn(normed, w_pad[:, wide(h)])
            q_ref[:, wide(h)] = (product * (SCALE * LOG2E) + row).astype(bf16)

    start = info[2 + sum(weights) + j]
    where = lax.broadcasted_iota(jnp.int32, (rows, 1), 0) + start
    bias = jnp.where((start < 0) | (where < info[1]), 0.0, MASKED)
    lane = lax.broadcasted_iota(jnp.int32, (rows, WIDE), 1)
    mark = jnp.where(lane == HEAD, bias, 0.0)
    for h in range(PAIR):
        k_ref[:, wide(h)] = (nn(normed, w_pad[:, wide(PAIR + h)]) + mark).astype(bf16)
        row = tail(vb_ref[:, part(h)], 1.0)
        v_ref[:, wide(h)] = (nn(normed, w_pad[:, wide(2 * PAIR + h)]) + row).astype(bf16)


def span_spec(shape, rows, low, count, grouped):
    inside = lambda j: jnp.clip(j - low, 0, count - 1)
    if grouped:
        return pl.BlockSpec((1, rows, shape[-1]), lambda j, info: (info[0], inside(j), 0))
    return pl.BlockSpec((rows, shape[-1]), lambda j, info: (inside(j), 0))


def project(fresh, info, sources, weights, q_bias, v_bias, rows, own, total):
    width = sources[0].shape[-1]
    last = own // rows - 1
    cols = PAIR * WIDE
    spans, specs = [], []
    for x in sources:
        low = spans[-1][1] if spans else 0
        count = x.shape[-2] // rows
        spans.append((low, low + count))
        specs.append(span_spec(x.shape, rows, low, count, x.ndim == 3))
    shapes = [(own, cols), (total, cols), (total, cols)] + ([(total, width)] if fresh else [])
    outs = [pl.BlockSpec((rows, cols), lambda j, info: (jnp.minimum(j, last), 0))]
    outs += [pl.BlockSpec((rows, s[1]), lambda j, info: (j, 0)) for s in shapes[1:]]
    outs += [whole((8, width))] if fresh else []
    flat = [q_bias, v_bias]
    return pl.pallas_call(
        functools.partial(project_kernel, fresh, own, spans, [w.shape[0] for w in weights]),
        grid_spec=pltpu.PrefetchScalarGridSpec(
            num_scalar_prefetch=1,
            grid=(total // rows,),
            in_specs=specs + [once(w.shape) for w in weights] + [whole(a.shape) for a in flat],
            out_specs=outs,
            scratch_shapes=[
                pltpu.VMEM((width, 3 * PAIR * WIDE), bf16),
                pltpu.VMEM((width, 128), f32),
            ],
        ),
        out_shape=[jax.ShapeDtypeStruct(s, bf16) for s in shapes]
        + ([jax.ShapeDtypeStruct((8, width), f32)] if fresh else []),
        compiler_params=params(),
        cost_estimate=cost(14 * total * width * cols, 8 * total * width),
    )(info, *sources, *weights, *flat)


def causal(count):
    row = lax.broadcasted_iota(jnp.int32, (count, count), 0)
    return row >= lax.broadcasted_iota(jnp.int32, (count, count), 1)


def attend_kernel(later, cont, q_ref, k_ref, v_ref, o_ref, log_ref):
    j = pl.program_id(0)
    rows = q_ref.shape[0]
    lanes = lax.broadcasted_iota(jnp.int32, (rows, 128), 1)

    def run(is_later):
        logs = jnp.zeros((rows, 128), f32)
        outs = []
        for h in range(PAIR):
            q = q_ref[:, wide(h)]
            scores = nt(q, k_ref[later:, wide(h)])
            top = jnp.max(scores, axis=1, keepdims=True)
            if is_later:
                near = []
                for i in range(rows // cont):
                    at = pl.ds(pl.multiple_of(j * rows + i * cont, cont), cont)
                    block = nt(q[i * cont : (i + 1) * cont], k_ref[at, wide(h)])
                    near.append(jnp.where(causal(cont), block, MASKED))
                near = jnp.concatenate(near, axis=0)
                top = jnp.maximum(top, jnp.max(near, axis=1, keepdims=True))
            out = nn(jnp.exp2(scores - top).astype(bf16), v_ref[later:, wide(h)])
            if is_later:
                near = jnp.exp2(near - top).astype(bf16)
                extra = []
                for i in range(rows // cont):
                    at = pl.ds(pl.multiple_of(j * rows + i * cont, cont), cont)
                    extra.append(nn(near[i * cont : (i + 1) * cont], v_ref[at, wide(h)]))
                out = out + jnp.concatenate(extra, axis=0)
            total = out[:, HEAD : HEAD + 1]
            outs.append(out[:, :HEAD] * (1.0 / total))
            logs = jnp.where(lanes == h, top + jnp.log2(total), logs)
        o_ref[...] = jnp.concatenate(outs, axis=1).astype(bf16)
        log_ref[...] = logs

    pl.when(j * rows < later)(lambda: run(True))
    pl.when(j * rows >= later)(lambda: run(False))


def attend(q, k, v, later, cont):
    own, cols = q.shape
    rows = min(512, later, own - later)
    block = lambda n: pl.BlockSpec((rows, n), lambda j: (j, 0))
    return pl.pallas_call(
        functools.partial(attend_kernel, later, cont),
        grid=(own // rows,),
        in_specs=[block(cols), whole(k.shape), whole(v.shape)],
        out_specs=[block(PAIR * HEAD), block(128)],
        out_shape=[
            jax.ShapeDtypeStruct((own, PAIR * HEAD), bf16),
            jax.ShapeDtypeStruct((own, 128), f32),
        ],
        compiler_params=params(),
        cost_estimate=cost(8 * own * k.shape[0] * cols // 2, 8 * own * cols),
    )(q, k, v)


def attend_back_kernel(
    later, cont, first, q_ref, k_ref, v_ref, o_ref, log_ref, g_ref, dq_ref, dk_ref, dv_ref, dk, dv
):
    j = pl.program_id(0)
    rows = q_ref.shape[0]

    @pl.when(j == 0)
    def _():
        dk[...] = jnp.zeros_like(dk)
        dv[...] = jnp.zeros_like(dv)

    def run(is_later):
        outs = []
        for h in range(PAIR):
            q = q_ref[:, wide(h)]
            log = log_ref[:, h : h + 1]
            g = g_ref[:, part(first + h)].astype(f32)
            inner = jnp.sum(g * o_ref[:, part(h)].astype(f32), axis=1, keepdims=True)
            g = tail(g, 0.0).astype(bf16)
            k = k_ref[later:, wide(h)]
            probs = jnp.exp2(nt(q, k) - log)
            drift = (probs * (nt(g, v_ref[later:, wide(h)]) - inner)).astype(bf16)
            dv[later:, wide(h)] += tn(probs.astype(bf16), g)
            dk[later:, wide(h)] += tn(drift, q)
            dq = nn(drift, k)
            if is_later:
                extra = []
                for i in range(rows // cont):
                    at = pl.ds(pl.multiple_of(j * rows + i * cont, cont), cont)
                    mine = slice(i * cont, (i + 1) * cont)
                    k = k_ref[at, wide(h)]
                    probs = jnp.where(causal(cont), jnp.exp2(nt(q[mine], k) - log[mine]), 0.0)
                    drift = nt(g[mine], v_ref[at, wide(h)]) - inner[mine]
                    drift = (probs * drift).astype(bf16)
                    dv[at, wide(h)] += tn(probs.astype(bf16), g[mine])
                    dk[at, wide(h)] += tn(drift, q[mine])
                    extra.append(nn(drift, k))
                dq = dq + jnp.concatenate(extra, axis=0)
            outs.append(dq[:, :HEAD] * SCALE)
        dq_ref[...] = jnp.concatenate(outs, axis=1).astype(bf16)

    pl.when(j * rows < later)(lambda: run(True))
    pl.when(j * rows >= later)(lambda: run(False))

    @pl.when(j == pl.num_programs(0) - 1)
    def _():
        outs = [dk[:, h * WIDE : h * WIDE + HEAD] * (1.0 / LOG2E) for h in range(PAIR)]
        dk_ref[...] = jnp.concatenate(outs, axis=1).astype(bf16)
        outs = [dv[:, h * WIDE : h * WIDE + HEAD] for h in range(PAIR)]
        dv_ref[...] = jnp.concatenate(outs, axis=1).astype(bf16)


def attend_back(q, k, v, out, logs, grad, first, later, cont):
    own, cols = q.shape
    total = k.shape[0]
    dense = PAIR * HEAD
    rows = min(512, later, own - later)
    block = lambda n: pl.BlockSpec((rows, n), lambda j: (j, 0))
    return pl.pallas_call(
        functools.partial(attend_back_kernel, later, cont, first),
        grid=(own // rows,),
        in_specs=[block(cols), whole(k.shape), whole(v.shape), block(dense), block(128), block(grad.shape[1])],
        out_specs=[block(dense), whole((total, dense)), whole((total, dense))],
        out_shape=[
            jax.ShapeDtypeStruct((own, dense), bf16),
            jax.ShapeDtypeStruct((total, dense), bf16),
            jax.ShapeDtypeStruct((total, dense), bf16),
        ],
        scratch_shapes=[pltpu.VMEM((total, cols), f32)] * 2,
        compiler_params=params(),
        cost_estimate=cost(1000, 1000),
    )(q, k, v, out, logs, grad)


WEIGHTS = 3


def middle_kernel(counts, info, tok_ref, go_ref, valid_ref, *refs):
    a_refs, refs = refs[:4], refs[4:]
    w_refs, refs = refs[: 4 * len(counts)], refs[4 * len(counts) :]
    ub_ref, y_ref, gm_ref, near_ref, far_ref, sum_ref, keep_ref, send_ref = refs[:8]
    w, acc, att, columns, vectors, sem = refs[8:]
    j = pl.program_id(0)
    cols = a_refs[0].shape[1]
    half = 2 * cols

    @pl.when(j == 0)
    def _():
        acc[...] = jnp.zeros_like(acc)
        sum_ref[...] = jnp.zeros_like(sum_ref)
        for r in range(4):
            spot = 1
            for w_ref in w_refs[r * len(counts) : (r + 1) * len(counts)]:
                count, deep = w_ref.shape[:2]
                for b in range(count):
                    at = pl.ds(pl.multiple_of(info[spot], 16), deep)
                    spot += 1
                    for m in range(WEIGHTS):
                        w[m, at, r * cols : (r + 1) * cols] = w_ref[
                            b, :, m * cols : (m + 1) * cols
                        ]
                    if r == 0:
                        columns[at, 0:4] = w_ref[b, :, 3 * cols : 3 * cols + 4].astype(f32)
        vectors[...] = columns[...].T[:8]

    for r in range(4):
        att[:, r * cols : (r + 1) * cols] = a_refs[r][...]
    attended = att[...]
    mixed = tok_ref[...].astype(f32) + nt(attended, w[0]) + vectors[2:3, :]
    unit, inverse = normalise(mixed)
    gain = vectors[0:1, :]
    normed = (unit * gain + vectors[1:2, :]).astype(bf16)
    upper = nn(normed, w[1]) + ub_ref[...]
    cumulative = 0.5 + 0.5 * lax.erf(upper * (0.5**0.5))
    active = (upper * cumulative).astype(bf16)
    output = mixed + nt(active, w[2]) + vectors[3:4, :]
    y_ref[...] = output.astype(bf16)
    sum_ref[0:1, :] += jnp.sum(output * output * valid_ref[...], axis=0, keepdims=True)

    go = go_ref[...]
    acc[2] += tn(go, active)
    density = jnp.exp(-0.5 * upper * upper) * (1.0 / math.sqrt(2.0 * math.pi))
    grad_upper = nn(go, w[2]) * (cumulative + upper * density)
    sum_ref[5:6, :] += jnp.sum(grad_upper, axis=0, keepdims=True)
    low = grad_upper.astype(bf16)
    acc[1] += tn(normed, low)
    grad_mid = nt(low, w[1])
    sum_ref[2:3, :] += jnp.sum(grad_mid * unit, axis=0, keepdims=True)
    sum_ref[3:4, :] += jnp.sum(grad_mid, axis=0, keepdims=True)
    grad_out = go.astype(f32)
    sum_ref[1:2, :] += jnp.sum(grad_out, axis=0, keepdims=True)
    grad_mixed = grad_out + norm_back(grad_mid, unit, inverse, gain)
    sum_ref[4:5, :] += jnp.sum(grad_mixed, axis=0, keepdims=True)
    gm_ref[...] = grad_mixed
    low = grad_mixed.astype(bf16)
    acc[0] += tn(low, attended)
    grad_attended = nn(low, w[0]).astype(bf16)
    near_ref[...] = grad_attended[:, :half]
    far_ref[...] = grad_attended[:, half:]

    @pl.when(j == pl.num_programs(0) - 1)
    def _():
        copies = []
        for m in range(WEIGHTS):
            w[m] = acc[m].astype(bf16)
            for i, out_ref in enumerate((keep_ref, send_ref)):
                source = w.at[m, :, pl.ds(i * half, half)]
                target = out_ref.at[:, pl.ds(m * half, half)]
                copies.append(pltpu.make_async_copy(source, target, sem.at[2 * m + i]))
                copies[-1].start()
        for copy in copies:
            copy.wait()


def middle(info, tokens, grad, valid, mine, theirs, weights, up_bias, rows, half):
    count, width = tokens.shape
    cols = mine[0].shape[1]
    per = half // rows
    block = lambda n: pl.BlockSpec((rows, n), lambda j, info: (j, 0))
    own = pl.BlockSpec(
        (rows, cols), lambda j, info: ((2 * (j // per) + info[0]) * per + j % per, 0)
    )
    flat = [w for group in weights for w in group]
    hbm = pl.BlockSpec(memory_space=pl.ANY)
    shape = jax.ShapeDtypeStruct
    return pl.pallas_call(
        functools.partial(middle_kernel, [w.shape[0] for w in weights[0]]),
        grid_spec=pltpu.PrefetchScalarGridSpec(
            num_scalar_prefetch=1,
            grid=(count // rows,),
            in_specs=[block(width), block(width), block(1), own, own, block(cols), block(cols)]
            + [once(w.shape) for w in flat]
            + [whole(up_bias.shape)],
            out_specs=[block(width), block(width), block(2 * cols), block(2 * cols)]
            + [whole((8, width)), hbm, hbm],
            scratch_shapes=[
                pltpu.VMEM((WEIGHTS, width, 4 * cols), bf16),
                pltpu.VMEM((WEIGHTS, width, 4 * cols), f32),
                pltpu.VMEM((rows, 4 * cols), bf16),
                pltpu.VMEM((width, 128), f32),
                pltpu.VMEM((8, width), f32),
                pltpu.SemaphoreType.DMA((2 * WEIGHTS,)),
            ],
        ),
        out_shape=[
            shape((count, width), bf16),
            shape((count, width), f32),
            shape((count, 2 * cols), bf16),
            shape((count, 2 * cols), bf16),
            shape((8, width), f32),
            shape((width, 2 * WEIGHTS * cols), bf16),
            shape((width, 2 * WEIGHTS * cols), bf16),
        ],
        compiler_params=params(),
        cost_estimate=cost(148 * count * width * cols, 30 * count * width),
    )(info, tokens, grad, valid, *mine, *theirs, *flat, up_bias)


BEYOND, BEYOND_TOO, THEIRS, MINE = 0, 1, 2, 3


def project_back_kernel(sums, spans, more, adding, placing, counts, info, *refs):
    x_ref, dq_ref, dk_ref, dv_ref = refs[:4]
    refs = refs[4:]
    w_refs, refs = refs[: len(counts)], refs[len(counts) :]
    prev_refs, refs = refs[:more], refs[more:]
    other, refs = refs[:adding], refs[adding:]
    shares, refs = refs[:placing], refs[placing:]
    outs, refs = refs[: len(spans)], refs[len(spans) :]
    d = refs[-3] if placing else refs[-1]
    j = pl.program_id(0)
    cols = dq_ref.shape[1]
    if spans:
        w = refs[-2]

        @pl.when(j == 0)
        def _():
            spot = 1
            for w_ref in w_refs:
                count, deep = w_ref.shape[:2]
                for b in range(count):
                    at = pl.ds(pl.multiple_of(info[spot], 16), deep)
                    w[at, : 3 * cols] = w_ref[b, :, : 3 * cols]
                    spot += 1
            w[:, 3 * cols :] = jnp.zeros_like(w[:, 3 * cols :])

    @pl.when(j == 0)
    def _():
        d[:, 3 * cols :] = jnp.zeros_like(d[:, 3 * cols :])

    asked = info[1 + sum(counts)]

    @pl.when(j < asked)
    def _():
        d[:, :cols] = jnp.zeros_like(dq_ref)

    @pl.when(j >= asked)
    def _():
        d[:, :cols] = dq_ref[...]

    d[:, cols : 2 * cols] = dk_ref[...]
    d[:, 2 * cols : 3 * cols] = dv_ref[...]
    all_d = d[...]
    if sums:
        dw_refs, refs = refs[:sums], refs[sums:]
        if placing:
            targets, (stage, sem) = refs[1:3], refs[-2:]
            refs = (refs[0], *refs[3:-2])
            half = stage.shape[1]
            c, y = info[0], info[2 + sum(counts)]
            loads, stores = [], []
            for i, share in enumerate(shares):
                spot = pl.ds(pl.multiple_of((c ^ (i % 2)) * half, 16), half)
                for kind, target in enumerate(targets):
                    n = 2 * i + kind
                    source, place = share.at[pl.ds(kind * half, half)], stage.at[n]
                    loads.append(pltpu.make_async_copy(source, place, sem.at[0, n]))
                    place = target.at[y ^ (i // 2), spot]
                    stores.append(pltpu.make_async_copy(stage.at[n], place, sem.at[1, n]))

            @pl.when(j == 0)
            def _():
                for copy in loads:
                    copy.start()

            @pl.when(j == 2)
            def _():
                for load, store in zip(loads, stores):
                    load.wait()
                    store.start()

            @pl.when(j == pl.num_programs(0) - 1)
            def _():
                for copy in stores:
                    copy.wait()

        sum_ref, acc = refs[:2]

        @pl.when(j == 0)
        def _():
            acc[...] = jnp.zeros_like(acc)
            sum_ref[...] = jnp.zeros_like(sum_ref)

        acc[...] += tn(x_ref[...], all_d)
        sum_ref[0:1, :] += jnp.sum(all_d.astype(f32), axis=0, keepdims=True)

        @pl.when(j == pl.num_programs(0) - 1)
        def _():
            at = 0
            for piece in other:
                acc[:, at : at + piece.shape[1]] += piece[...].astype(f32)
                at += piece.shape[1]
            at = 0
            for dw_ref in dw_refs:
                dw_ref[...] = acc[:, at : at + dw_ref.shape[1]].astype(bf16)
                at += dw_ref.shape[1]

    if spans:
        grad = nt(all_d, w[...])
        for i, (low, high) in enumerate(spans):

            @pl.when((j >= low) & (j < high))
            def _():
                if more:
                    outs[i][...] = (grad + prev_refs[i][...].astype(f32)).astype(bf16)
                else:
                    outs[i][...] = grad.astype(bf16)


def tiled(count):
    return -(-count // 256) * 256


def project_back(
    sums, wanted, c, y, starts, x, dq, dk, dv, weights, previous, rows, half, own, other, shares
):
    total, width = x.shape
    cols = dq.shape[1]
    sizes = ((total - own) // 2 // rows,) * 2 + (own // 2 // rows,) * 2
    n_beyond = 2 * sizes[0] if BEYOND in wanted else 0
    n_half = sizes[2]
    per = half // rows
    steps = sum(sizes[i] for i in wanted)
    info = jnp.stack([jnp.asarray(v, jnp.int32) for v in (c, *starts, n_beyond, y)])

    def row(j, info):
        i = j - n_beyond
        share = (i >= n_half).astype(jnp.int32)
        i = i - share * n_half
        side = jnp.where(share == 1, info[0], 1 - info[0])
        inner = (2 * (i // per) + side) * per + i % per
        return jnp.where(j < n_beyond, own // rows + j, inner)

    def dq_row(j, info):
        return jnp.minimum(row(jnp.maximum(j, n_beyond), info), own // rows - 1)

    x_spec = pl.BlockSpec((rows, width), lambda j, info: (row(j, info), 0))
    d_spec = pl.BlockSpec((rows, cols), lambda j, info: (row(j, info), 0))
    q_spec = pl.BlockSpec((rows, cols), lambda j, info: (dq_row(j, info), 0))
    parts, spans, low = [], [], 0
    if previous is not None:
        for i in wanted:
            n = sizes[i]
            spans.append((low, low + n))
            parts.append(
                pl.BlockSpec(
                    (rows, width),
                    functools.partial(lambda a, b, j, info: (jnp.clip(j - a, 0, b - 1), 0), low, n),
                )
            )
            low += n
    shape = jax.ShapeDtypeStruct
    out_specs = list(parts)
    out_shape = [shape((sizes[i] * rows, width), bf16) for i in wanted[: len(parts)]]
    scratch = []
    lanes = tiled(3 * cols)
    if sums:
        out_specs += [whole((width, n)) for n in sums] + [whole((8, lanes))]
        out_shape += [shape((width, n), bf16) for n in sums] + [shape((8, lanes), f32)]
        scratch.append(pltpu.VMEM((width, lanes), f32))
    hbm = pl.BlockSpec(memory_space=pl.ANY)
    if shares:
        out_specs += [hbm, hbm]
        out_shape += [shape((2, own // 2, width), bf16)] * 2
    if parts:
        scratch.append(pltpu.VMEM((width, lanes), bf16))
    scratch.append(pltpu.VMEM((rows, lanes), bf16))
    if shares:
        scratch.append(pltpu.VMEM((2 * len(shares), half, width), bf16))
        scratch.append(pltpu.SemaphoreType.DMA((2, 2 * len(shares))))
    return pl.pallas_call(
        functools.partial(
            project_back_kernel,
            len(sums),
            spans,
            len(previous or []),
            len(other),
            len(shares),
            [w.shape[0] for w in weights],
        ),
        grid_spec=pltpu.PrefetchScalarGridSpec(
            num_scalar_prefetch=1,
            grid=(steps,),
            in_specs=[x_spec, q_spec, d_spec, d_spec]
            + [once(w.shape) for w in weights]
            + (parts if previous else [])
            + [once(o.shape) for o in other]
            + [hbm] * len(shares),
            out_specs=out_specs,
            scratch_shapes=scratch,
        ),
        out_shape=out_shape,
        compiler_params=params(),
        cost_estimate=cost(1000, 1000),
    )(info, x, dq, dk, dv, *weights, *(previous or []), *other, *shares)


def finish_kernel(n, gain_ref, tok_ref, mix_ref, *refs):
    shares, (low_ref, sum_ref) = refs[:n], refs[n:]

    @pl.when(pl.program_id(0) == 0)
    def _():
        sum_ref[...] = jnp.zeros_like(sum_ref)

    grad = shares[0][...].astype(f32)
    for share in shares[1:]:
        grad = grad + share[...].astype(f32)
    unit, inverse = normalise(tok_ref[...].astype(f32))
    back = norm_back(grad, unit, inverse, gain_ref[0:1, :])
    low_ref[...] = (mix_ref[...] + back).astype(bf16)
    sum_ref[0:1, :] += jnp.sum(grad * unit, axis=0, keepdims=True)
    sum_ref[1:2, :] += jnp.sum(grad, axis=0, keepdims=True)


def finish(kind, gain, tokens, mixed, shares, back, half):
    width = tokens.shape[1]
    rows = min(128, half)
    n = half // rows
    block = pl.BlockSpec((rows, width), lambda j: (kind * n + j, 0))
    plain = pl.BlockSpec((rows, width), lambda j: (j, 0))
    return pl.pallas_call(
        functools.partial(finish_kernel, len(shares) + len(back)),
        grid=(n,),
        in_specs=[whole(gain.shape), block, block] + [block] * len(shares) + [plain] * len(back),
        out_specs=[plain, whole((8, width))],
        out_shape=[
            jax.ShapeDtypeStruct((half, width), bf16),
            jax.ShapeDtypeStruct((8, width), f32),
        ],
        compiler_params=params(),
        cost_estimate=cost(1000, 1000),
    )(gain, tokens, mixed, *shares, *back)


def assemble_kernel(count, info, *refs):
    i = pl.program_id(0)
    for m in range(count):

        @pl.when(i == m)
        def _():
            refs[-1][...] = refs[m][...].astype(refs[-1].dtype)[None]


def assemble(info, pieces, kind, half, dtype, first=0, into=()):
    width = pieces[0].shape[1]
    count = len(pieces)
    return pl.pallas_call(
        functools.partial(assemble_kernel, count),
        grid_spec=pltpu.PrefetchScalarGridSpec(
            num_scalar_prefetch=1,
            grid=(count,),
            in_specs=[pl.BlockSpec((half, width), lambda i, info: (kind, 0))] * count
            + [pl.BlockSpec(memory_space=pl.ANY)] * len(into),
            out_specs=pl.BlockSpec(
                (1, half, width),
                lambda i, info: (info[0] ^ ((first + i) // 2), info[1] ^ ((first + i) % 2), 0),
            ),
        ),
        out_shape=jax.ShapeDtypeStruct((2, 2 * half, width), dtype),
        input_output_aliases={count + 1: 0} if into else {},
        compiler_params=params(),
        cost_estimate=cost(1000, 1000),
    )(info, *pieces, *into)


def rows_kernel(n, one_ref, two_ref, *outs):
    for i, out in enumerate(outs):
        out[...] = one_ref[i, :] if i < n else two_ref[i - n, :]


def rows_of(one, two):
    shapes = [(one.shape[1],)] * one.shape[0] + [(two.shape[1],)] * two.shape[0]
    return pl.pallas_call(
        functools.partial(rows_kernel, one.shape[0]),
        out_shape=[jax.ShapeDtypeStruct(s, f32) for s in shapes],
        cost_estimate=cost(1000, 1000),
    )(one, two)


def swap(value, axis, bit):
    count = lax.axis_size(axis)
    return lax.ppermute(value, axis, [(i, i ^ bit) for i in range(count)])


def pick(array, index, axis=0):
    return lax.dynamic_index_in_dim(array, index, axis, keepdims=False)


def in_order(index, mine, theirs, axis=0):
    first = index == 0
    return jnp.stack(
        [jnp.where(first, mine, theirs), jnp.where(first, theirs, mine)], axis=axis
    )


def direct():
    return lax.axis_size(C) == 2 and lax.axis_size(S) == 4


def phase(*values):
    return lax.optimization_barrier(values)


def over_z(piece):
    return [swap(piece, S, i) for i in (1, 2, 3)]


def z_parts(rows, axis):
    z = lax.axis_index(S)
    low = rows.astype(bf16)
    return [pick(low, z ^ i, axis) for i in (1, 2, 3)], pick(rows, z, axis)


def z_sum(mine, parts):
    for piece in parts:
        mine = mine + piece.astype(f32)
    return mine


def z_moves(parts):
    return [swap(piece, S, i + 1) for i, piece in enumerate(parts)]


def x_parts(rows, axis):
    x = lax.axis_index(C)
    shape = rows.shape
    split = rows.reshape(*shape[:axis], 4, 2, shape[axis] // 8, *shape[axis + 1 :])
    return pick(split, 1 - x, axis + 1).astype(bf16), pick(split, x, axis + 1)


def sum_over(values, axis):
    count, bit = lax.axis_size(axis), 1
    while bit < count:
        values = values + swap(values, axis, bit)
        bit *= 2
    return values


def body(
    prompt_tokens,
    later_tokens,
    prompt_upstream,
    later_upstream,
    prompt_lengths,
    later_lengths,
    query_weight,
    key_weight,
    value_weight,
    out_weight,
    up_weight,
    down_weight,
    pre_gain,
    pre_shift,
    mid_gain,
    mid_shift,
    query_bias,
    value_bias,
    out_bias,
    up_bias,
    down_bias,
):
    groups, prompt_rows, width = prompt_tokens.shape
    count, cont = later_tokens.shape[1:3]
    later = count * cont
    own = later + prompt_rows
    contexts = lax.axis_size(C)
    total = later + prompt_rows * contexts
    cols = query_weight.shape[1]
    half = later // 2
    big = min(512, later)
    x = lax.axis_index(C)
    t = lax.axis_index(T)
    y, c = t // 2, t % 2
    turn = (t, t ^ 2, t ^ 1, t ^ 3)

    def share(array, side):
        rows = array.reshape(2, 2, half, array.shape[-1])
        return pick(rows, side, 1).reshape(2 * half, array.shape[-1])

    prompt = pick(prompt_tokens, y)
    qkv_piece = jnp.concatenate(
        [query_weight, key_weight, value_weight, pre_gain[:, None], pre_shift[:, None]], axis=1
    )
    oud_piece = jnp.concatenate(
        [out_weight.T, up_weight, down_weight.T]
        + [v[:, None] for v in (mid_gain, mid_shift, out_bias, down_bias)],
        axis=1,
    )
    length = pick(prompt_lengths, y)
    lengths = pick(later_lengths, y)
    follow = pick(later_tokens, y).reshape(later, width)
    row_tokens = share(jnp.concatenate([follow, prompt], axis=0), c)
    later_valid = jnp.arange(cont, dtype=jnp.int32)[None, :] < lengths[:, None]
    prompt_valid = x * prompt_rows + jnp.arange(prompt_rows, dtype=jnp.int32) < length
    valid = jnp.concatenate([later_valid.reshape(later), prompt_valid]).astype(f32)
    valid = share(valid[:, None], c)
    upstream = jnp.concatenate(
        [pick(later_upstream, y).reshape(later, width), pick(prompt_upstream, y)], axis=0
    )
    grad_low = (share(upstream, c).astype(f32) * valid).astype(bf16)

    biases = jnp.concatenate([query_bias, value_bias, up_bias])[None]
    if direct():
        z = lax.axis_index(S)
        deep = query_weight.shape[0]
        starts = [((z ^ i) * 2 + (x ^ k)) * deep for k in (0, 1) for i in range(4)]
        places = [(1 - x) * prompt_rows + side * half for side in (c, 1 - c)]
        tokens_piece = pick(prompt_tokens.reshape(groups * 2, half, width), 2 * y + c)
        tokens_piece, qkv_piece = phase(tokens_piece, qkv_piece)
        tokens_piece = swap(tokens_piece, C, 1)
        parts = over_z(qkv_piece)
        rows = jnp.pad(biases, ((0, 15), (0, qkv_piece.shape[1] - biases.shape[1])))
        far_piece = swap(jnp.concatenate([qkv_piece, rows]), T, 2)
        far_piece, tokens_piece, oud_piece, row_tokens, grad_low, valid, *parts = phase(
            far_piece, tokens_piece, oud_piece, row_tokens, grad_low, valid, *parts
        )
        far_biases = far_piece[deep : deep + 1, : biases.shape[1]]
        far_piece = far_piece[:deep]
        near = jnp.stack([qkv_piece, *parts])
        qkv_own = [near, swap(near, C, 1)]
        beyond = [tokens_piece, swap(tokens_piece, T, 1)]
        parts = [far_piece, *over_z(far_piece)]
        parts = phase(*qkv_own, *beyond, *parts, oud_piece)
        qkv_own, beyond, oud_piece = list(parts[:2]), list(parts[2:4]), parts[8]
        near = jnp.stack(parts[4:8])
        qkv_far = [near, swap(near, C, 1)]
        oud_parts = over_z(oud_piece)
    else:
        starts = [0]
        rolled = jnp.roll(lax.all_gather(prompt, C), -x, axis=0)[1:]
        beyond = [rolled.reshape(-1, width)]
        places = [((x + i) % contexts) * prompt_rows for i in range(1, contexts)]
        qkv_own = [lax.all_gather(qkv_piece, SC, axis=0, tiled=True)[None]]
        qkv_far = [swap(w, T, 2) for w in qkv_own]
        far_biases = swap(biases, T, 2)
    biases = jnp.concatenate([biases, far_biases]).astype(f32)

    def ints(*values):
        return jnp.stack([jnp.asarray(v, jnp.int32) for v in values])

    blocks = [-1] * (later // big)
    blocks += [x * prompt_rows + i * big for i in range(prompt_rows // big)]
    blocks += [p + i * big for p in places for i in range(max(half if direct() else prompt_rows, big) // big)]
    info = ints(y, length, *starts, *blocks)

    q0, k0, v0, normed_in, pre_vectors = project(
        True,
        info,
        [later_tokens.reshape(groups, later, width), prompt_tokens] + beyond,
        qkv_own,
        biases[0:1, :cols],
        biases[0:1, cols : 2 * cols],
        big,
        own,
        total,
    )
    if direct():
        q0, k0, v0, normed_in, *parts = phase(q0, k0, v0, normed_in, *qkv_far, *oud_parts)
        qkv_far = parts[:2]
        near = jnp.stack([oud_piece, *parts[2:]])
        oud_own = [near, swap(near, C, 1)]
        near = swap(near, T, 2)
    a0, log0 = attend(q0, k0, v0, later, cont)
    if direct():
        a0, near, *oud_own = phase(a0, near, *oud_own)
        oud_far = [near, swap(near, C, 1)]
    else:
        oud_own = [lax.all_gather(oud_piece, SC, axis=0, tiled=True)[None]]
        oud_far = [swap(w, T, 2) for w in oud_own]
    oud = [oud_own, oud_far] + [[swap(w, T, 1) for w in ws] for ws in (oud_own, oud_far)]
    r0 = swap(share(a0, 1 - c), T, 1)
    up_bias = biases[:, 2 * cols :]
    up_bias = jnp.concatenate([up_bias, swap(up_bias, T, 1)]).reshape(1, -1)
    q1, k1, v1 = project(
        False,
        info,
        [normed_in],
        qkv_far,
        biases[1:2, :cols],
        biases[1:2, cols : 2 * cols],
        big,
        own,
        total,
    )
    if direct():
        q1, k1, v1, oud[2][0], oud[2][1], oud[3][0], r0, up_bias = phase(
            q1, k1, v1, oud[2][0], oud[2][1], oud[3][0], r0, up_bias
        )
    a1, log1 = attend(q1, k1, v1, later, cont)
    if direct():
        a1, oud_far[1] = phase(a1, oud_far[1])
        oud[3][1] = swap(oud_far[1], T, 1)
    r1 = swap(share(a1, 1 - c), T, 1)

    output, grad_mixed, grad_near, grad_away, sums, oud_keep, oud_send = middle(
        ints(c, *starts),
        row_tokens,
        grad_low,
        valid,
        [a0, a1],
        [r0, r1],
        oud,
        up_bias,
        min(256, half),
        half,
    )

    where = ints(y, c)
    back_rows = min(512, half)
    everything = (BEYOND, BEYOND_TOO, THEIRS, MINE)
    lanes = tiled(3 * cols)
    far_widths = (3 * lanes // 4, lanes // 4)
    received = swap(grad_away, T, 1)
    grad_heads = in_order(
        c, grad_near.reshape(2, half, -1), received.reshape(2, half, -1), 1
    ).reshape(own, -1)
    if direct():
        grad_heads, oud_send, output = phase(grad_heads, oud_send, output)
    oud_send = swap(oud_send, T, 1)
    outputs = [output, swap(output, T, 1), swap(output, T, 2), None]

    def back_from(q, k, v, out, logs, weights, first):
        def run(grads):
            return attend_back(q, k, v, out, logs, grads, first, later, cont)

        def inputs(grads, wanted, widths, previous, other=(), shares=()):
            return project_back(
                widths,
                wanted,
                c,
                y,
                starts,
                normed_in,
                *grads,
                weights,
                previous,
                back_rows,
                half,
                own,
                other,
                shares,
            )

        return run, inputs

    far_attend, far_back = back_from(q1, k1, v1, a1, log1, qkv_far, PAIR)
    near_attend, near_back = back_from(q0, k0, v0, a0, log0, qkv_own, 0)

    grads = far_attend(grad_heads)
    if direct():
        *grads, oud_keep, oud_send = phase(*grads, oud_keep, oud_send)
    oud_parts = [slice(0, min(1024, oud_send.shape[1])), slice(min(1024, oud_send.shape[1]), None)]
    oud_parts = [oud_keep[:, p].astype(f32) + oud_send[:, p].astype(f32) for p in oud_parts]
    if direct():
        away, kept = zip(*[x_parts(p, 0) for p in oud_parts])
        kept = [k.astype(bf16) for k in kept]
        *grads, kept[0], kept[1], away0, away1 = phase(*grads, *kept, *away)
        away0 = swap(away0, C, 1)
    *shares, far, far_rest, sums1 = far_back(grads, everything, far_widths, [])
    if direct():
        far, far_rest, grad_heads, away0, away1, outputs[1], outputs[2] = phase(
            far, far_rest, grad_heads, away0, away1, outputs[1], outputs[2]
        )
        parts, first_sum = z_parts(kept[0].astype(f32) + away0.astype(f32), 0)
        grad_heads, far, away1, first_sum, *parts = phase(grad_heads, far, away1, first_sum, *parts)
        away1 = swap(away1, C, 1)
        first_parts = z_moves(parts)
    far = swap(far, T, 2)
    grads = near_attend(grad_heads)
    if direct():
        *grads, far, far_rest, away1, first_sum, outputs[2], p1, p2, p3 = phase(
            *grads, far, far_rest, away1, first_sum, outputs[2], *first_parts
        )
        first_done = [p1, p2, p3]
        parts, last_sum = z_parts(kept[1].astype(f32) + away1.astype(f32), 0)
        g0, far_rest, first_sum, last_sum, *parts = phase(
            grads[0], far_rest, first_sum, last_sum, *parts
        )
        grads[0] = g0
        last_parts = z_moves(parts)
    far_rest = swap(far_rest, T, 2)
    outputs[3] = swap(outputs[2], T, 1)
    if direct():
        b0, b1, their_share, my_share = near_back(grads, everything, (), shares)
        b0, b1, their_share, my_share, first_sum, last_sum, far, far_rest, *parts = phase(
            b0,
            b1,
            their_share,
            my_share,
            first_sum,
            last_sum,
            far,
            far_rest,
            grads[0],
            outputs[3],
            *first_done,
            *last_parts,
        )
        grads[0], outputs[3] = parts[:2]
        their_share, b1 = swap(their_share, T, 1), swap(b1, T, 1)
        first_sum, last_sum = z_sum(first_sum, parts[2:5]), z_sum(last_sum, parts[5:])
        oud_grad = jnp.concatenate([first_sum, last_sum], axis=1).astype(bf16)
        oud_far = oud_grad.reshape(-1, WEIGHTS, 2, cols)[:, :, 1]
        my_share, their_share, b0, b1, oud_grad, oud_far = phase(
            my_share, their_share, b0, b1, oud_grad, oud_far
        )
        oud_far = swap(oud_far, T, 2)
        back = swap((b0.astype(f32) + b1.astype(f32)).astype(bf16), C, 1)
        shares = [my_share, their_share]
        low, sums_later = finish(0, pre_vectors, row_tokens, grad_mixed, shares, [], half)
        low, sums_later, shares[0], shares[1], oud_far, far, far_rest, g0, *outputs = phase(
            low, sums_later, *shares, oud_far, far, far_rest, grads[0], *outputs
        )
        grads[0] = g0
        pieces = [low, swap(low, T, 1), swap(low, T, 2), None]
        widths = (5 * lanes // 8, 3 * lanes // 8)
        *near, sums0, later_output, prompt_output = near_back(
            grads, everything, widths, None, (far, far_rest), outputs
        )
        x_away, x_kept = x_parts(near[0], 0)
        z_split = near[1].reshape(4, 2 * deep, widths[1])
        parts, z_kept = [pick(z_split, z ^ i) for i in (1, 2, 3)], pick(z_split, z)
        x_away, x_kept, z_kept, sums0, pieces[1], *parts = phase(
            x_away, x_kept, z_kept, sums0, pieces[1], *parts
        )
        x_away = swap(x_away, C, 1)
        z_away = z_moves(parts)
        back, pieces[2] = phase(back, pieces[2])
        pieces[3] = swap(pieces[2], T, 1)
        low, sums_prompt = finish(1, pre_vectors, row_tokens, grad_mixed, shares, [back], half)
    else:
        oud_grad = jnp.concatenate([p.astype(bf16) for p in oud_parts], axis=1)
        b0, b1, their_share, my_share, near, sums0 = near_back(
            grads, everything, (lanes,), shares, (far, far_rest)
        )
        shares = [my_share, swap(their_share, T, 1)]
        back = jnp.concatenate([b0, b1])
        back = back.astype(f32) + swap(back, T, 1).astype(f32)
        back = back.reshape(contexts - 1, prompt_rows, width)
        back = jnp.concatenate([jnp.zeros_like(back[:1]), back], axis=0)
        back = jnp.roll(back, x, axis=0).astype(bf16)
        back = lax.psum_scatter(back, C, scatter_dimension=0, tiled=True)
        back = pick(back.reshape(2, half, width), c)
        low, sums_later = finish(0, pre_vectors, row_tokens, grad_mixed, shares, [], half)
        pieces = [low, None, swap(low, T, 2), None]
        low, sums_prompt = finish(1, pre_vectors, row_tokens, grad_mixed, shares, [back], half)
        later_output = assemble(where, outputs, 0, half, bf16)
        prompt_output = assemble(where, outputs, 1, half, bf16)
        qkv_grad, oud_grad = [
            lax.psum_scatter(g, SC, scatter_dimension=0, tiled=True) for g in (near, oud_grad)
        ]
        qkv_grad = qkv_grad.astype(f32)

    def placed(*pieces):
        block = lax.broadcasted_iota(jnp.int32, (lax.axis_size(T), cols), 0)
        return sum(jnp.where(block == i, v[None], 0.0) for i, v in zip(turn, pieces)).reshape(-1)

    row = lax.broadcasted_iota(jnp.int32, (8, width), 0)
    lane = lax.broadcasted_iota(jnp.int32, (8, width), 1)
    group = lax.axis_index(S) * groups + y
    every = lax.axis_size(S) * groups
    scalars = jnp.where(lane == group, jnp.sum(sums[0]), 0.0)
    scalars = jnp.where(lane == every + group, jnp.sum(valid), scalars)
    up_sums = placed(*sums[5].reshape(4, cols))
    sums = jnp.where(row == 6, scalars, jnp.where(row == 7, up_sums[None], sums))
    q_sums = placed(sums0[0, :cols], sums1[0, :cols])
    v_sums = placed(sums0[0, 2 * cols : 3 * cols], sums1[0, 2 * cols : 3 * cols])
    more = jnp.where(row == 2, q_sums[None], jnp.where(row == 3, v_sums[None], sums_later))
    if direct():
        low, sums_prompt, sums, more, oud_grad, oud_far, x_away, x_kept, z_kept, *rest = phase(
            low,
            sums_prompt,
            sums,
            more,
            oud_grad,
            oud_far,
            x_away,
            x_kept,
            z_kept,
            *pieces,
            *z_away,
        )
        pieces, z_away = rest[:4], rest[4:]
    sums = jnp.concatenate([sums, more + sums_prompt])
    sums = sums + swap(sums, T, 2)
    if direct():
        low, sums = phase(low, sums)
    last = [low, swap(low, T, 1), swap(low, T, 2), None]
    if direct():
        z_first = z_sum(z_kept.astype(f32), z_away).reshape(2, deep, widths[1])
        z_away, z_first = pick(z_first, 1 - x).astype(bf16), pick(z_first, x)
        parts, x_first = z_parts(x_kept.astype(f32) + x_away.astype(f32), 0)
        z_away, z_first, x_first, pieces[0], *parts = phase(
            z_away, z_first, x_first, pieces[0], *parts
        )
        parts = z_moves(parts)
        later_grad = assemble(where, pieces, 0, half, f32)
        later_grad, sums, last[1], z_away, x_first, *parts = phase(
            later_grad, sums, last[1], z_away, x_first, *parts
        )
        z_away = swap(z_away, C, 1)
        sums = sums + swap(sums, T, 1)
        sums, last[1], x_first, *parts = phase(sums, last[1], x_first, *parts)
        arrived = swap(sums, C, 1)
        prompt_grad = assemble(where, last[:2], 0, half, f32)
        qkv_grad = jnp.concatenate(
            [z_sum(x_first, parts), z_first + z_away.astype(f32)], axis=1
        )
        sums = sum_over(sums + arrived, S)
        prompt_grad, sums, last[2], qkv_grad = phase(prompt_grad, sums, last[2], qkv_grad)
    else:
        pieces[1] = swap(pieces[0], T, 1)
        pieces[3] = swap(pieces[2], T, 1)
        later_grad = assemble(where, pieces, 0, half, f32)
        prompt_grad = assemble(where, last[:2], 0, half, f32)
        sums = sum_over(sum_over(sums + swap(sums, T, 1), C), S)
    oud_grad = oud_grad.reshape(-1, WEIGHTS, 2, cols)
    if not direct():
        oud_far = swap(oud_grad[:, :, 1], T, 2)
    oud_grad = oud_grad[:, :, 0].astype(f32) + oud_far.astype(f32)
    last[3] = swap(last[2], T, 1)
    squares = lax.dynamic_slice(sums[6], (lax.axis_index(S) * groups,), (groups,))
    counted = lax.dynamic_slice(sums[6], (every + lax.axis_index(S) * groups,), (groups,))
    magnitude = jnp.sqrt(squares / (counted * width))
    prompt_grad = assemble(where, last[2:], 0, half, f32, 2, [prompt_grad])
    n = width // (lax.axis_size(S) * contexts)
    place = lax.axis_index(S) * contexts + x

    vectors = lax.dynamic_slice(sums, (0, place * n), (10, n))
    heads = lax.dynamic_slice(sums, (7, t * cols), (5, cols))
    rows = rows_of(vectors, heads)
    shaped = (groups, count, cont, width)
    return (
        prompt_output,
        later_output.reshape(shaped),
        prompt_grad,
        later_grad.reshape(shaped),
        qkv_grad[:, :cols],
        qkv_grad[:, cols : 2 * cols],
        qkv_grad[:, 2 * cols : 3 * cols],
        oud_grad[:, 0].T,
        oud_grad[:, 1],
        oud_grad[:, 2].T,
        rows[8],
        rows[9],
        rows[2],
        rows[3],
        rows[13],
        rows[14],
        rows[4],
        rows[10],
        rows[1],
        magnitude,
    )


def solution(mesh):
    rows, later, vector = P(S, C, None), P(S, C, None, None), P(SC)
    weight, turned, column = P(SC, T), P(T, SC), P(T)
    return jax.shard_map(
        body,
        mesh=mesh,
        in_specs=(rows, later, rows, later, P(S), P(S, C))
        + (weight, weight, weight, turned, weight, turned)
        + (vector,) * 4
        + (column, column, vector, column, vector),
        out_specs=(rows, later, rows, later)
        + (weight, weight, weight, turned, weight, turned)
        + (vector,) * 4
        + (column, column, vector, column, vector, P(S)),
        check_vma=False,
    )
```
